32 devices in a mesh: group: 2 (over y), expert: 4 (over z), replica: 2 (over x), learner: 2 (over core).
Axes of the slice: x: 2, y: 2, z: 4, core: 2. Of those that a mesh axis runs over, the one named last changes fastest.
Arguments:
- tokens: bfloat16 [4, 256, 4096], P(None, ('group', 'expert', 'learner')), parts along dimension 1, may hold values from -6 to 6
- gates: float32 [4, 256, 2], P(None, ('group', 'expert', 'learner')), parts along dimension 1, may hold values from 0.05 to 1
- expert_ids: int32 [4, 256, 2], P(None, ('group', 'expert', 'learner')), parts along dimension 1, may hold values from 0 to 3, as said below
- gate_up_tiles: bfloat16 [4, 4096, 2, 1536], P(None, ('expert', 'learner'), None, 'replica'), may hold values from -4 to 4
- gate_up_scales: float32 [4, 32, 2, 12], replicated, may hold values from 0.0078125 to 0.03125
- down_tiles: bfloat16 [4, 1536, 4096], P(None, ('expert', 'learner'), 'replica'), may hold values from -4 to 4
- down_scales: float32 [4, 12, 32], replicated, may hold values from 0.02 to 0.1
Outputs:
- layer_out: bfloat16 [4, 256, 4096], P(None, ('group', 'expert', 'learner'), 'replica'), parts along dimension 1
The draws below stay inside these ranges and needn't reach their ends.
There are 2 independent parts, one for each index of `group`. The reference program is written for one: setup_inputs(seed, part) draws one part's arguments, and reference() takes and returns one part's arrays. A program takes and returns all parts, laid end to end along the dimension named above; an argument that names none is the same for every part. Nothing has to cross between parts.
Inputs may be any that keep to these rules, and one draw needn't show every extreme that they name: `expert_ids`: each row names 2 different experts. Within the rows of one device in one micro-batch (aligned blocks of 16 rows), no expert is named by more than 12 rows; in every micro-batch some expert is named by exactly 12 rows of every device.
All inputs are finite; a program needn't handle non-finite values.
Results may differ from the reference program's by a relative error of at most 0.0076.
Values may be sent and summed in bfloat16 or wider, within the bound.
A program may use at most 128 MiB of HBM per device.

```python
import math
import jax
import jax.numpy as jnp
from jax import lax

D = 4096
F = 1536
TILE = 128
STEPS = 4
ROWS_DEV = 16
EXPERTS = 4
TOPK = 2
ROWS = 128
CAP = 12


def draw_expert_ids(key, part):
    key = jax.random.fold_in(key, 7)
    per_batch = ROWS // ROWS_DEV
    blocks = STEPS * per_batch
    others = EXPERTS - 1
    subkeys = jax.random.split(key, 5)
    hot_expert = jax.random.randint(subkeys[0], (STEPS,), 0, EXPERTS)
    hot_rows = jnp.repeat(hot_expert, per_batch, total_repeat_length=blocks)[:, None, None]
    block_shift = jax.random.randint(subkeys[1], (blocks,), 0, others)[:, None, None]
    other_order = jax.vmap(lambda key_part: jax.random.permutation(key_part, others))(jax.random.split(subkeys[2], blocks))
    row_rank = jax.vmap(lambda key_part: jax.random.permutation(key_part, ROWS_DEV))(jax.random.split(subkeys[3], blocks))
    slot_roll = jax.random.randint(subkeys[4], (blocks, ROWS_DEV, 1), 0, TOPK)
    row_ids = jnp.arange(ROWS_DEV, dtype=jnp.int32)
    row_base = row_ids * others // ROWS_DEV
    has_hot = (row_rank < CAP).astype(jnp.int32)[:, :, None]
    slot_ids = jnp.arange(TOPK, dtype=jnp.int32)
    window_pos = (block_shift + row_base[None, :, None] + slot_ids[None, None, :] - has_hot) % others
    spread_order = jnp.broadcast_to(other_order[:, None, :], (blocks, ROWS_DEV, others))
    picked = jnp.take_along_axis(spread_order, window_pos, axis=2)
    expert = (hot_rows + 1 + picked) % EXPERTS
    expert = jnp.where((has_hot == 1) & (slot_ids[None, None, :] == 0), hot_rows, expert)
    rolled = (slot_ids[None, None, :] + slot_roll) % TOPK
    expert = jnp.take_along_axis(expert, rolled, axis=2)
    return expert.reshape(STEPS, ROWS, TOPK).astype(jnp.int32)


def shard_levels(key, dims, shards, least, largest):
    def one(dim, shards_of):
        heights = jax.random.uniform(jax.random.fold_in(jax.random.fold_in(key, 6), dim), (shards_of,), jnp.float32, least / len(shards), largest / len(shards))
        return jnp.repeat(jnp.exp(heights), dims[dim] // shards_of).reshape((-1,) + (1,) * (len(dims) - dim - 1))

    gain = one(*shards[0])
    for cut in shards[1:]:
        gain = gain * one(*cut)
    return gain


def scatter_about(stream_key, dims, width, limit, shards=(), kind=jnp.bfloat16):
    factor_of = shard_levels(stream_key, dims, shards, -0.22, 0.18) if shards else 1.0
    entries = jax.random.normal(stream_key, dims, jnp.float32) * width * factor_of
    return jnp.minimum(jnp.maximum(entries, -limit), limit).astype(kind)


def setup_inputs(seed: int = 0, part: int = 0) -> dict:
    arg_keys = jax.random.split(jax.random.key(seed), 8)
    part_keys = jax.random.split(jax.random.fold_in(arg_keys[7], part), 8)
    return {
        "tokens": scatter_about(part_keys[0], (STEPS, ROWS, D), 1.0, 6.0, ((1, 8),)),
        "gates": jnp.clip(jnp.exp(math.log(1.0) - 2.9957323 * jax.random.uniform(part_keys[1], (STEPS, ROWS, TOPK), jnp.float32) ** shard_levels(part_keys[1], (STEPS, ROWS, TOPK), ((1, 8),), -0.2, 0.2)), 0.05, 1.0),
        "expert_ids": draw_expert_ids(jax.random.fold_in(jax.random.fold_in(arg_keys[7], part), 71), part),
        "gate_up_tiles": scatter_about(arg_keys[3], (EXPERTS, D, 2, F), 1.0, 4.0, ((1, 8), (3, 2))),
        "gate_up_scales": jnp.clip(jnp.exp(jax.random.uniform(arg_keys[4], (EXPERTS, D // TILE, 2, F // TILE), jnp.float32, math.log(0.0078125), math.log(0.03125))), 0.0078125, 0.03125),
        "down_tiles": scatter_about(arg_keys[5], (EXPERTS, F, D), 1.0, 4.0, ((1, 8), (2, 2))),
        "down_scales": jnp.clip(jnp.exp(jax.random.uniform(arg_keys[6], (EXPERTS, F // TILE, D // TILE), jnp.float32, math.log(0.02), math.log(0.1))), 0.02, 0.1),
    }


def dequant(tile_values, scales, first_axis, second_axis):
    grown = jnp.repeat(jnp.repeat(scales, TILE, axis=first_axis), TILE, axis=second_axis)
    return (tile_values.astype(jnp.float32) * grown).astype(jnp.bfloat16)


def reference(tokens, gates, expert_ids, gate_up_tiles, gate_up_scales, down_tiles, down_scales):
    gate_share = gates / jnp.sum(gates, axis=2, keepdims=True)
    row_limit = (ROWS // ROWS_DEV) * CAP
    step_ids = jnp.arange(STEPS, dtype=jnp.int32)[:, None]

    def one_expert(running, expert_index):
        tiles_gate_up = lax.dynamic_index_in_dim(gate_up_tiles, expert_index, 0, keepdims=False)
        scales_gate_up = lax.dynamic_index_in_dim(gate_up_scales, expert_index, 0, keepdims=False)
        w_gate_up = dequant(tiles_gate_up, scales_gate_up, 0, 2).reshape(D, 2 * F)
        tiles_down = lax.dynamic_index_in_dim(down_tiles, expert_index, 0, keepdims=False)
        scales_down = lax.dynamic_index_in_dim(down_scales, expert_index, 0, keepdims=False)
        w_down = dequant(tiles_down, scales_down, 0, 1)
        chosen = expert_ids == expert_index
        weight = jnp.sum(jnp.where(chosen, gate_share, 0.0), axis=2)
        named = jnp.any(chosen, axis=2)
        row_order = jnp.argsort(jnp.where(named, 0, 1).astype(jnp.int32), axis=1, stable=True)
        row_order = row_order[:, :row_limit].astype(jnp.int32)
        picked_rows = tokens[step_ids, row_order].reshape(STEPS * row_limit, D)
        gate_up_out = jnp.dot(picked_rows, w_gate_up, preferred_element_type=jnp.float32)
        hidden = (jax.nn.silu(gate_up_out[:, :F]) * gate_up_out[:, F:]).astype(jnp.bfloat16)
        expert_out = jnp.dot(hidden, w_down, preferred_element_type=jnp.float32).astype(jnp.bfloat16)
        expert_out = lax.optimization_barrier(expert_out).astype(jnp.float32).reshape(STEPS, row_limit, D)
        picked_weight = weight[step_ids, row_order]
        running = running.at[step_ids, row_order].add(picked_weight[:, :, None] * expert_out)
        return running, None

    running, _ = lax.scan(one_expert, jnp.zeros((STEPS, ROWS, D), jnp.float32), jnp.arange(EXPERTS, dtype=jnp.int32))
    return running.astype(jnp.bfloat16)
```

```python
import jax
import jax.numpy as jnp
from jax import lax
from jax.sharding import PartitionSpec as P

ROW_AXES = ("expert", "learner")


def body(tokens, gates, expert_ids, gate_up_tiles, gate_up_scales, down_tiles, down_scales):
    steps, rows_dev, width = tokens.shape
    top = expert_ids.shape[2]
    n_z = lax.axis_size("expert")
    n_c = lax.axis_size("learner")
    n_x = lax.axis_size("replica")
    n_dev = n_z * n_c
    z, c, x = lax.axis_index("expert"), lax.axis_index("learner"), lax.axis_index("replica")
    me = z * n_c + c
    experts, d_loc, _, units = gate_up_tiles.shape
    f_loc, cols = down_tiles.shape[1:]
    tile = width // gate_up_scales.shape[1]
    piece = units // n_dev
    f32, bf16 = jnp.float32, jnp.bfloat16

    xs = lax.all_to_all(tokens, ROW_AXES, split_axis=2, concat_axis=1, tiled=True)
    n_rows = steps * rows_dev * n_dev
    xs = xs.reshape(n_rows, d_loc)
    share = gates / jnp.sum(gates, axis=2, keepdims=True)
    route = jnp.concatenate([expert_ids.astype(f32), share], axis=2)
    route = lax.all_gather(route, ROW_AXES, axis=1, tiled=True).reshape(n_rows, 2 * top)
    ids = route[:, :top].T.astype(jnp.int32)
    share = route[:, top:].T

    def take(scales, axis, first, count):
        index = (first + jnp.arange(count)) // tile
        onehot = (index[:, None] == jnp.arange(scales.shape[axis])[None, :]).astype(f32)
        return jnp.moveaxis(
            jnp.tensordot(scales, onehot, axes=([axis], [1]), precision=lax.Precision.HIGHEST), -1, axis
        )

    s1 = take(take(gate_up_scales, 1, me * d_loc, d_loc), 3, x * units, units)
    w1 = (gate_up_tiles.astype(f32) * s1).astype(bf16).reshape(experts * d_loc, 2 * units)
    s2 = take(take(down_scales, 1, me * f_loc, f_loc), 2, x * cols, cols)
    w2 = (down_tiles.astype(f32) * s2).astype(bf16).reshape(experts * f_loc, cols)

    names = jnp.arange(experts, dtype=jnp.int32)
    picked = ids[:, :, None] == names
    masked = jnp.where(picked[..., None], xs[None, :, None, :], jnp.zeros((), bf16))
    part = jnp.dot(masked.reshape(top * n_rows, experts * d_loc), w1, preferred_element_type=f32)
    part = part.astype(bf16).reshape(top * n_rows, 2, n_z, n_c, piece)

    def core_sum(value, axis):
        mine = lax.dynamic_index_in_dim(value, c, axis, keepdims=False)
        other = lax.dynamic_index_in_dim(value, 1 - c, axis, keepdims=False)
        got = lax.ppermute(other, "learner", [(0, 1), (1, 0)])
        return (mine.astype(f32) + got.astype(f32)).astype(bf16)

    half = jnp.moveaxis(core_sum(part, 3), 2, 0)
    got = lax.all_to_all(half, "expert", split_axis=0, concat_axis=0, tiled=True)
    total = jnp.sum(got.astype(f32), axis=0)
    hidden = jax.nn.silu(total[:, 0]) * total[:, 1]
    hidden = (hidden * share.reshape(-1)[:, None]).astype(bf16)

    pieces = []
    for turn in range(n_x):
        pairs = []
        for zz in range(n_z):
            for xx in range(n_x):
                for cc in range(n_c):
                    q = zz * n_c + cc
                    owner = (n_dev // n_x) * xx + q // n_x
                    source = (zz * n_x + xx) * n_c + cc
                    target = (owner // n_c * n_x + (q + turn) % n_x) * n_c + owner % n_c
                    pairs.append((source, target))
        pieces.append(lax.ppermute(hidden, ("expert", "replica", "learner"), pairs))
    stack = jnp.stack(pieces)
    order = jnp.mod(x - jnp.arange(n_x), n_x)
    ordered = jnp.take(stack, order, axis=0)
    h = jnp.moveaxis(ordered, 0, 1).reshape(top, n_rows, f_loc)
    wide = jnp.zeros((n_rows, experts, f_loc), bf16)
    for k in range(top):
        wide = wide + jnp.where(picked[k][..., None], h[k][:, None, :], jnp.zeros((), bf16))
    out = jnp.dot(wide.reshape(n_rows, experts * f_loc), w2, preferred_element_type=f32)
    out = out.astype(bf16).reshape(steps, n_z, n_c, rows_dev, cols)
    half = jnp.moveaxis(core_sum(out, 2), 1, 0)
    got = lax.all_to_all(half, "expert", split_axis=0, concat_axis=0, tiled=True)
    return jnp.sum(got.astype(f32), axis=0).astype(bf16)


def solution(mesh):
    placed = (
        P(None, ("group", "expert", "learner"), None),
        P(None, ("group", "expert", "learner"), None),
        P(None, ("group", "expert", "learner"), None),
        P(None, ("expert", "learner"), None, "replica"),
        P(),
        P(None, ("expert", "learner"), "replica"),
        P(),
    )
    return jax.shard_map(
        body,
        mesh=mesh,
        in_specs=placed,
        out_specs=P(None, ("group", "expert", "learner"), "replica"),
        check_vma=False,
    )
```

```python
import functools

import jax
import jax.numpy as jnp
from jax import lax
from jax.experimental import pallas as pl
from jax.experimental.pallas import tpu as pltpu
from jax.sharding import PartitionSpec as P

ROW_AXES = ("expert", "learner")
LANE = 128
OUT_COLS = 512


def shift(index, by, count):
    return lax.rem(index + by, count)


def kernel(sizes, xs, route, w1, w2, out, xm, s_send, s_recv, own, z_send, z_recv, hid, h_recv,
           wide, q_send, q_recv, q_own, o_send, o_recv,
           s_ss, s_rs, z_ss, z_rs, h_ss, h_rs, q_ss, q_rs, o_ss, o_rs):
    n_z, n_x, top, experts, rows, d_loc, f_loc, span = sizes
    n_c = 2
    f32, bf16 = jnp.float32, jnp.bfloat16
    z, c, x = lax.axis_index("expert"), lax.axis_index("learner"), lax.axis_index("replica")
    me = z * n_c + c
    chunks = w1.shape[0]
    slots = top * rows
    per_plane = n_z * n_c // n_x
    sibling = {"learner": 1 - c}

    def remote(src, dst, send, recv, device):
        return pltpu.make_async_remote_copy(
            src_ref=src, dst_ref=dst, send_sem=send, recv_sem=recv,
            device_id=device, device_id_type=pl.DeviceIdType.MESH)

    barrier = pltpu.get_barrier_semaphore()
    everyone = n_z * n_c * n_x
    here = (z * n_x + x) * n_c + c
    for turn in range(1, everyone):
        there = shift(here, turn, everyone)
        pl.semaphore_signal(
            barrier, inc=1,
            device_id={"expert": there // (n_x * n_c), "replica": there // n_c % n_x, "learner": there % n_c},
            device_id_type=pl.DeviceIdType.MESH)

    def block_of(half, zz):
        return zz * n_c + (c if half else 1 - c)

    for half in range(2):
        for zz in range(n_z):
            p = block_of(half, zz)
            ids = route[p]
            value = xs[p]
            for k in range(top):
                name = jnp.broadcast_to(ids[:, k:k + 1], (rows, d_loc))
                for e in range(experts):
                    xm[half, zz * slots + k * rows:zz * slots + (k + 1) * rows, e * d_loc:(e + 1) * d_loc] = (
                        jnp.where(name == e, value.astype(f32), 0.0).astype(bf16))
    pl.semaphore_wait(barrier, everyone - 1)

    def sib_copy(n):
        return remote(s_send.at[n], s_recv.at[n], s_ss.at[n], s_rs.at[n], sibling)

    def z_copy(n, turn):
        to = shift(z, turn, n_z)
        return remote(z_send.at[n, to], z_recv.at[n, z], z_ss.at[n, to], z_rs.at[n, z], {"expert": to})

    def z_arrival(n, turn):
        source = shift(z, turn, n_z)
        return remote(z_send.at[n, source], z_recv.at[n, source], z_ss.at[n, source], z_rs.at[n, source], {"expert": source})

    def finish(n):
        sib_copy(n).wait_recv()
        both = own[lax.rem(n, 2)] + s_recv[n].astype(f32)
        z_send[n] = both.astype(bf16).reshape(n_z, slots, 2 * LANE)
        for turn in range(1, n_z):
            z_copy(n, turn).start()

    def step(n, carry):
        s_send[n] = jnp.dot(xm[0], w1[n], preferred_element_type=f32).astype(bf16)
        sib_copy(n).start()
        own[lax.rem(n, 2)] = jnp.dot(xm[1], w1[n], preferred_element_type=f32)

        @pl.when(n > 0)
        def _():
            finish(n - 1)
        return carry

    lax.fori_loop(0, chunks, step, 0)
    finish(chunks - 1)

    mine = route[me]

    def h_copy(jj, xx):
        owner = per_plane * x + jj
        first = jj * f_loc // LANE
        return remote(hid.at[pl.ds(first, span)], h_recv.at[me], h_ss.at[jj, xx], h_rs.at[me],
                      {"expert": owner // n_c, "learner": owner % n_c, "replica": xx})

    def is_me(jj, xx):
        return (per_plane * x + jj == me) & (x == xx)

    for n in range(chunks):
        total = z_send[n, z].astype(f32)
        for turn in range(1, n_z):
            z_arrival(n, turn).wait_recv()
        for turn in range(1, n_z):
            total = total + z_recv[n, shift(z, turn, n_z)].astype(f32)
        gate, up = total[:, :LANE], total[:, LANE:]
        value = gate / (1.0 + jnp.exp(-gate)) * up
        for k in range(top):
            part = value[k * rows:(k + 1) * rows] * mine[:, top + k:top + k + 1]
            hid[n, k * rows:(k + 1) * rows, :] = part.astype(bf16)
        for jj in range(per_plane):
            first = jj * f_loc // LANE
            if first + span - 1 != n:
                continue
            for xx in range(n_x):
                @pl.when(jnp.logical_not(is_me(jj, xx)))
                def _(jj=jj, xx=xx):
                    h_copy(jj, xx).start()

                @pl.when(is_me(jj, xx))
                def _(first=first):
                    h_recv[me] = hid[first:first + span]

    source_x = me // per_plane
    for p in range(n_z * n_c):
        @pl.when(jnp.logical_not((p == me) & (source_x == x)))
        def _(p=p):
            remote(hid.at[pl.ds(0, span)], h_recv.at[p], h_ss.at[0, 0], h_rs.at[p],
                   {"expert": p // n_c, "learner": p % n_c, "replica": source_x}).wait_recv()

    depth = span * LANE
    for half in range(2):
        for zz in range(n_z):
            p = block_of(half, zz)
            ids = route[p]
            for e in range(experts):
                for s in range(span):
                    value = jnp.zeros((rows, LANE), f32)
                    for k in range(top):
                        name = jnp.broadcast_to(ids[:, k:k + 1], (rows, LANE))
                        value = value + jnp.where(name == e, h_recv[p, s, k * rows:(k + 1) * rows, :].astype(f32), 0.0)
                    wide[half, zz * rows:(zz + 1) * rows, e * depth + s * LANE:e * depth + (s + 1) * LANE] = value.astype(bf16)

    def q_copy(n):
        return remote(q_send.at[n], q_recv.at[n], q_ss.at[n], q_rs.at[n], sibling)

    def o_copy(n, turn):
        to = shift(z, turn, n_z)
        return remote(o_send.at[n, to], o_recv.at[n, z], o_ss.at[n, to], o_rs.at[n, z], {"expert": to})

    def o_arrival(n, turn):
        source = shift(z, turn, n_z)
        return remote(o_send.at[n, source], o_recv.at[n, source], o_ss.at[n, source], o_rs.at[n, source], {"expert": source})

    def finish_out(n):
        q_copy(n).wait_recv()
        both = q_own[lax.rem(n, 2)] + q_recv[n].astype(f32)
        o_send[n] = both.astype(bf16).reshape(n_z, rows, OUT_COLS)
        for turn in range(1, n_z):
            o_copy(n, turn).start()

    out_chunks = w2.shape[1] // OUT_COLS

    def step_out(n, carry):
        columns = pl.ds(pl.multiple_of(n * OUT_COLS, OUT_COLS), OUT_COLS)
        q_send[n] = jnp.dot(wide[0], w2[:, columns], preferred_element_type=f32).astype(bf16)
        q_copy(n).start()
        q_own[lax.rem(n, 2)] = jnp.dot(wide[1], w2[:, columns], preferred_element_type=f32)

        @pl.when(n > 0)
        def _():
            finish_out(n - 1)
        return carry

    lax.fori_loop(0, out_chunks, step_out, 0)
    finish_out(out_chunks - 1)

    for n in range(out_chunks):
        total = o_send[n, z].astype(f32)
        for turn in range(1, n_z):
            o_arrival(n, turn).wait_recv()
        for turn in range(1, n_z):
            total = total + o_recv[n, shift(z, turn, n_z)].astype(f32)
        out[:, n * OUT_COLS:(n + 1) * OUT_COLS] = total.astype(bf16)

    for n in range(chunks):
        sib_copy(n).wait_send()
        for turn in range(1, n_z):
            z_copy(n, turn).wait_send()
    for jj in range(per_plane):
        for xx in range(n_x):
            @pl.when(jnp.logical_not(is_me(jj, xx)))
            def _(jj=jj, xx=xx):
                h_copy(jj, xx).wait_send()
    for n in range(out_chunks):
        q_copy(n).wait_send()
        for turn in range(1, n_z):
            o_copy(n, turn).wait_send()


def fused(sizes, xs, route, w1, w2):
    n_z, n_x, top, experts, rows, d_loc, f_loc, span = sizes
    n_dev = 2 * n_z
    chunks, cols = w1.shape[0], w2.shape[1]
    slots = top * rows
    out_chunks = cols // OUT_COLS
    bf16, f32 = jnp.bfloat16, jnp.float32
    vmem, dma = pltpu.VMEM, pltpu.SemaphoreType.DMA
    per_plane = n_dev // n_x
    return pl.pallas_call(
        functools.partial(kernel, sizes),
        out_shape=jax.ShapeDtypeStruct((rows, cols), bf16),
        in_specs=[pl.BlockSpec(memory_space=pltpu.VMEM)] * 4,
        out_specs=pl.BlockSpec(memory_space=pltpu.VMEM),
        scratch_shapes=[
            vmem((2, n_z * slots, experts * d_loc), bf16),
            vmem((chunks, n_z * slots, 2 * LANE), bf16),
            vmem((chunks, n_z * slots, 2 * LANE), bf16),
            vmem((2, n_z * slots, 2 * LANE), f32),
            vmem((chunks, n_z, slots, 2 * LANE), bf16),
            vmem((chunks, n_z, slots, 2 * LANE), bf16),
            vmem((chunks, slots, LANE), bf16),
            vmem((n_dev, span, slots, LANE), bf16),
            vmem((2, n_z * rows, experts * span * LANE), bf16),
            vmem((out_chunks, n_z * rows, OUT_COLS), bf16),
            vmem((out_chunks, n_z * rows, OUT_COLS), bf16),
            vmem((2, n_z * rows, OUT_COLS), f32),
            vmem((out_chunks, n_z, rows, OUT_COLS), bf16),
            vmem((out_chunks, n_z, rows, OUT_COLS), bf16),
            dma((chunks,)), dma((chunks,)),
            dma((chunks, n_z)), dma((chunks, n_z)),
            dma((per_plane, n_x)), dma((n_dev,)),
            dma((out_chunks,)), dma((out_chunks,)),
            dma((out_chunks, n_z)), dma((out_chunks, n_z)),
        ],
        compiler_params=pltpu.CompilerParams(
            collective_id=0, has_side_effects=True, vmem_limit_bytes=58 * 1024 * 1024),
    )(xs, route, w1, w2)


def kernel_sizes(n_z, n_c, n_x, top, experts, rows, d_loc, f_loc, units, cols):
    if n_c != 2 or units % LANE or cols % OUT_COLS or rows % 16 or (n_z * n_c) % n_x:
        return None
    spans = [-(-((j + 1) * f_loc) // LANE) - j * f_loc // LANE for j in range(n_z * n_c // n_x)]
    span = max(spans)
    chunks = units // LANE
    if any(j * f_loc // LANE + span > chunks for j in range(len(spans))):
        return None
    if 2 * n_z * top * rows * experts * d_loc * 2 > 8 * 1024 * 1024:
        return None
    return n_z, n_x, top, experts, rows, d_loc, f_loc, span


def plain(tokens, route, w1, w2, n_x):
    f32, bf16 = jnp.float32, jnp.bfloat16
    n_z, n_c = lax.axis_size("expert"), lax.axis_size("learner")
    c, x = lax.axis_index("learner"), lax.axis_index("replica")
    n_dev = n_z * n_c
    steps, rows_dev, _ = tokens.shape
    experts, d_loc, _, units = w1.shape
    f_loc, cols = w2.shape[1:]
    top = route.shape[2] // 2
    piece = units // n_dev
    n_rows = steps * rows_dev * n_dev
    xs = lax.all_to_all(tokens, ROW_AXES, split_axis=2, concat_axis=1, tiled=True).reshape(n_rows, d_loc)
    route = route.reshape(n_dev, steps, rows_dev, 2 * top).swapaxes(0, 1).reshape(n_rows, 2 * top)
    ids = route[:, :top].T.astype(jnp.int32)
    share = route[:, top:].T
    w1 = w1.reshape(experts * d_loc, 2 * units)
    w2 = w2.reshape(experts * f_loc, cols)
    names = jnp.arange(experts, dtype=jnp.int32)
    picked = ids[:, :, None] == names
    masked = jnp.where(picked[..., None], xs[None, :, None, :], jnp.zeros((), bf16))
    part = jnp.dot(masked.reshape(top * n_rows, experts * d_loc), w1, preferred_element_type=f32)
    part = part.astype(bf16).reshape(top * n_rows, 2, n_z, n_c, piece)

    def core_sum(value, axis):
        mine = lax.dynamic_index_in_dim(value, c, axis, keepdims=False)
        other = lax.dynamic_index_in_dim(value, 1 - c, axis, keepdims=False)
        got = lax.ppermute(other, "learner", [(0, 1), (1, 0)])
        return (mine.astype(f32) + got.astype(f32)).astype(bf16)

    half = jnp.moveaxis(core_sum(part, 3), 2, 0)
    got = lax.all_to_all(half, "expert", split_axis=0, concat_axis=0, tiled=True)
    total = jnp.sum(got.astype(f32), axis=0)
    hidden = jax.nn.silu(total[:, 0]) * total[:, 1]
    hidden = (hidden * share.reshape(-1)[:, None]).astype(bf16)

    pieces = []
    for turn in range(n_x):
        pairs = []
        for zz in range(n_z):
            for xx in range(n_x):
                for cc in range(n_c):
                    q = zz * n_c + cc
                    owner = (n_dev // n_x) * xx + q // n_x
                    source = (zz * n_x + xx) * n_c + cc
                    target = (owner // n_c * n_x + (q + turn) % n_x) * n_c + owner % n_c
                    pairs.append((source, target))
        pieces.append(lax.ppermute(hidden, ("expert", "replica", "learner"), pairs))
    stack = jnp.stack(pieces)
    order = jnp.mod(x - jnp.arange(n_x), n_x)
    ordered = jnp.take(stack, order, axis=0)
    h = jnp.moveaxis(ordered, 0, 1).reshape(top, n_rows, f_loc)
    wide = jnp.zeros((n_rows, experts, f_loc), bf16)
    for k in range(top):
        wide = wide + jnp.where(picked[k][..., None], h[k][:, None, :], jnp.zeros((), bf16))
    out = jnp.dot(wide.reshape(n_rows, experts * f_loc), w2, preferred_element_type=f32)
    out = out.astype(bf16).reshape(steps, n_z, n_c, rows_dev, cols)
    half = jnp.moveaxis(core_sum(out, 2), 1, 0)
    got = lax.all_to_all(half, "expert", split_axis=0, concat_axis=0, tiled=True)
    return jnp.sum(got.astype(f32), axis=0).astype(bf16)


def body(tokens, gates, expert_ids, gate_up_tiles, gate_up_scales, down_tiles, down_scales):
    steps, rows_dev, width = tokens.shape
    top = expert_ids.shape[2]
    n_z = lax.axis_size("expert")
    n_c = lax.axis_size("learner")
    n_x = lax.axis_size("replica")
    n_dev = n_z * n_c
    z, c, x = lax.axis_index("expert"), lax.axis_index("learner"), lax.axis_index("replica")
    me = z * n_c + c
    experts, d_loc, _, units = gate_up_tiles.shape
    f_loc, cols = down_tiles.shape[1:]
    tile = width // gate_up_scales.shape[1]
    f32, bf16 = jnp.float32, jnp.bfloat16

    def take(scales, axis, first, count):
        index = (first + jnp.arange(count)) // tile
        onehot = (index[:, None] == jnp.arange(scales.shape[axis])[None, :]).astype(f32)
        return jnp.moveaxis(
            jnp.tensordot(scales, onehot, axes=([axis], [1]), precision=lax.Precision.HIGHEST), -1, axis
        )

    s1 = take(take(gate_up_scales, 1, me * d_loc, d_loc), 3, x * units, units)
    w1 = (gate_up_tiles.astype(f32) * s1).astype(bf16)
    s2 = take(take(down_scales, 1, me * f_loc, f_loc), 2, x * cols, cols)
    w2 = (down_tiles.astype(f32) * s2).astype(bf16)


    rows = steps * rows_dev
    share = gates / jnp.sum(gates, axis=2, keepdims=True)
    route = jnp.concatenate([expert_ids.astype(f32), share], axis=2).reshape(1, rows, 2 * top)
    route = lax.all_gather(route, ROW_AXES, axis=0, tiled=True)
    sizes = kernel_sizes(n_z, n_c, n_x, top, experts, rows, d_loc, f_loc, units, cols)
    if sizes is None:
        return plain(tokens, route, w1, w2, n_x)
    xs = jnp.swapaxes(tokens.reshape(rows, n_dev, d_loc), 0, 1)
    xs = lax.all_to_all(xs, ROW_AXES, split_axis=0, concat_axis=0, tiled=True)
    route = jnp.pad(route, ((0, 0), (0, 0), (0, LANE - 2 * top)))
    w1 = w1.reshape(experts * d_loc, 2, units // LANE, LANE)
    w1 = w1.transpose(2, 0, 1, 3).reshape(units // LANE, experts * d_loc, 2 * LANE)
    depth = sizes[-1] * LANE
    offset = lax.rem(lax.rem(me, n_dev // n_x) * f_loc, LANE)
    options = sorted({j * f_loc % LANE for j in range(n_dev // n_x)})
    padded = 0
    for option in options:
        case = jnp.pad(w2, ((0, 0), (option, depth - f_loc - option), (0, 0)))
        padded = padded + jnp.where(offset == option, case, jnp.zeros((), bf16))
    out = fused(sizes, xs, route, w1, padded.reshape(experts * depth, cols))
    return out.reshape(steps, rows_dev, cols)


def solution(mesh):
    placed = (
        P(None, ("group", "expert", "learner"), None),
        P(None, ("group", "expert", "learner"), None),
        P(None, ("group", "expert", "learner"), None),
        P(None, ("expert", "learner"), None, "replica"),
        P(),
        P(None, ("expert", "learner"), "replica"),
        P(),
    )
    return jax.shard_map(
        body,
        mesh=mesh,
        in_specs=placed,
        out_specs=P(None, ("group", "expert", "learner"), "replica"),
        check_vma=False,
    )
```

```python
import functools

import jax
import jax.numpy as jnp
from jax import lax
from jax.experimental import pallas as pl
from jax.experimental.pallas import tpu as pltpu
from jax.sharding import PartitionSpec as P

ROW_AXES = ("expert", "learner")
LANE = 128
OUT_COLS = 512


def shift(index, by, count):
    return lax.rem(index + by, count)


def kernel(sizes, xs, my_route, w1_in, w2_in, out, route, w1, w2, xm, s_send, s_recv, own, z_send, z_recv, hid, h_recv,
           wide, q_send, q_recv, q_own, o_send, o_recv,
           w1_s, w2_s, r_ss, r_rs, s_ss, s_rs, z_ss, z_rs, h_ss, h_rs, q_ss, q_rs, o_ss, o_rs):
    n_z, n_x, top, experts, rows, d_loc, f_loc, span = sizes
    n_c = 2
    f32, bf16 = jnp.float32, jnp.bfloat16
    z, c, x = lax.axis_index("expert"), lax.axis_index("learner"), lax.axis_index("replica")
    me = z * n_c + c
    chunks = w1.shape[0]
    slots = top * rows
    per_plane = n_z * n_c // n_x
    sibling = {"learner": 1 - c}

    def remote(src, dst, send, recv, device):
        return pltpu.make_async_remote_copy(
            src_ref=src, dst_ref=dst, send_sem=send, recv_sem=recv,
            device_id=device, device_id_type=pl.DeviceIdType.MESH)

    depth = span * LANE

    def w1_copy(n, e, g):
        return pltpu.make_async_copy(
            w1_in.at[e, g, :, pl.ds(pl.multiple_of(n * LANE, LANE), LANE)],
            w1.at[n, pl.ds(e * d_loc, d_loc), pl.ds(g * LANE, LANE)], w1_s.at[n, e, g])

    offset = lax.rem(lax.rem(me, per_plane) * f_loc, LANE)

    def w2_copy(e):
        return pltpu.make_async_copy(
            w2_in.at[e], w2.at[pl.ds(pl.multiple_of(e * depth + offset, 16), f_loc)], w2_s.at[e])

    for n in range(chunks):
        for e in range(experts):
            for g in range(2):
                w1_copy(n, e, g).start()
    for e in range(experts):
        w2_copy(e).start()

    barrier = pltpu.get_barrier_semaphore()
    everyone = n_z * n_c * n_x
    here = (z * n_x + x) * n_c + c
    for turn in range(1, everyone):
        there = shift(here, turn, everyone)
        pl.semaphore_signal(
            barrier, inc=1,
            device_id={"expert": there // (n_x * n_c), "replica": there // n_c % n_x, "learner": there % n_c},
            device_id_type=pl.DeviceIdType.MESH)

    def block_of(half, zz):
        return zz * n_c + (c if half else 1 - c)

    pl.semaphore_wait(barrier, everyone - 1)
    blocks = n_z * n_c

    def route_copy(turn):
        to = shift(me, turn, blocks)
        return remote(my_route, route.at[me], r_ss.at[to], r_rs.at[me],
                      {"expert": to // n_c, "learner": to % n_c})

    def route_arrival(turn):
        source = shift(me, turn, blocks)
        return remote(my_route, route.at[source], r_ss.at[source], r_rs.at[source],
                      {"expert": source // n_c, "learner": source % n_c})

    for turn in range(1, blocks):
        route_copy(turn).start()
    route[me] = my_route[...]
    if depth > f_loc:
        gap = depth - f_loc
        for option in sorted({j * f_loc % LANE for j in range(per_plane)}):
            @pl.when(offset == option)
            def _(option=option):
                for e in range(experts):
                    if option:
                        w2[e * depth:e * depth + option] = jnp.zeros((option, w2.shape[1]), bf16)
                    if gap > option:
                        w2[e * depth + option + f_loc:(e + 1) * depth] = jnp.zeros((gap - option, w2.shape[1]), bf16)
    for turn in range(1, blocks):
        route_arrival(turn).wait_recv()

    for half in range(2):
        for zz in range(n_z):
            p = block_of(half, zz)
            ids = route[p]
            value = xs[p]
            for k in range(top):
                name = jnp.broadcast_to(ids[:, k:k + 1], (rows, d_loc))
                for e in range(experts):
                    xm[half, zz * slots + k * rows:zz * slots + (k + 1) * rows, e * d_loc:(e + 1) * d_loc] = (
                        jnp.where(name == e, value.astype(f32), 0.0).astype(bf16))

    def sib_copy(n):
        return remote(s_send.at[n], s_recv.at[n], s_ss.at[n], s_rs.at[n], sibling)

    def z_copy(n, turn):
        to = shift(z, turn, n_z)
        return remote(z_send.at[n, to], z_recv.at[n, z], z_ss.at[n, to], z_rs.at[n, z], {"expert": to})

    def z_arrival(n, turn):
        source = shift(z, turn, n_z)
        return remote(z_send.at[n, source], z_recv.at[n, source], z_ss.at[n, source], z_rs.at[n, source], {"expert": source})

    def finish(n):
        sib_copy(n).wait_recv()
        both = own[lax.rem(n, 2)] + s_recv[n].astype(f32)
        z_send[n] = both.astype(bf16).reshape(n_z, slots, 2 * LANE)
        for turn in range(1, n_z):
            z_copy(n, turn).start()

    def step(n, carry):
        for e in range(experts):
            for g in range(2):
                w1_copy(n, e, g).wait()
        s_send[n] = jnp.dot(xm[0], w1[n], preferred_element_type=f32).astype(bf16)
        sib_copy(n).start()
        own[lax.rem(n, 2)] = jnp.dot(xm[1], w1[n], preferred_element_type=f32)

        @pl.when(n > 0)
        def _():
            finish(n - 1)
        return carry

    lax.fori_loop(0, chunks, step, 0)
    finish(chunks - 1)

    mine = route[me]

    def h_copy(jj, xx):
        owner = per_plane * x + jj
        first = jj * f_loc // LANE
        return remote(hid.at[pl.ds(first, span)], h_recv.at[me], h_ss.at[jj, xx], h_rs.at[me],
                      {"expert": owner // n_c, "learner": owner % n_c, "replica": xx})

    def is_me(jj, xx):
        return (per_plane * x + jj == me) & (x == xx)

    for n in range(chunks):
        total = z_send[n, z].astype(f32)
        for turn in range(1, n_z):
            z_arrival(n, turn).wait_recv()
        for turn in range(1, n_z):
            total = total + z_recv[n, shift(z, turn, n_z)].astype(f32)
        gate, up = total[:, :LANE], total[:, LANE:]
        value = gate / (1.0 + jnp.exp(-gate)) * up
        for k in range(top):
            part = value[k * rows:(k + 1) * rows] * mine[:, top + k:top + k + 1]
            hid[n, k * rows:(k + 1) * rows, :] = part.astype(bf16)
        for jj in range(per_plane):
            first = jj * f_loc // LANE
            if first + span - 1 != n:
                continue
            for xx in range(n_x):
                @pl.when(jnp.logical_not(is_me(jj, xx)))
                def _(jj=jj, xx=xx):
                    h_copy(jj, xx).start()

                @pl.when(is_me(jj, xx))
                def _(first=first):
                    h_recv[me] = hid[first:first + span]

    source_x = me // per_plane
    for p in range(n_z * n_c):
        @pl.when(jnp.logical_not((p == me) & (source_x == x)))
        def _(p=p):
            remote(hid.at[pl.ds(0, span)], h_recv.at[p], h_ss.at[0, 0], h_rs.at[p],
                   {"expert": p // n_c, "learner": p % n_c, "replica": source_x}).wait_recv()

    for half in range(2):
        for zz in range(n_z):
            p = block_of(half, zz)
            ids = route[p]
            for e in range(experts):
                for s in range(span):
                    value = jnp.zeros((rows, LANE), f32)
                    for k in range(top):
                        name = jnp.broadcast_to(ids[:, k:k + 1], (rows, LANE))
                        value = value + jnp.where(name == e, h_recv[p, s, k * rows:(k + 1) * rows, :].astype(f32), 0.0)
                    wide[half, zz * rows:(zz + 1) * rows, e * depth + s * LANE:e * depth + (s + 1) * LANE] = value.astype(bf16)

    def q_copy(n):
        return remote(q_send.at[n], q_recv.at[n], q_ss.at[n], q_rs.at[n], sibling)

    def o_copy(n, turn):
        to = shift(z, turn, n_z)
        return remote(o_send.at[n, to], o_recv.at[n, z], o_ss.at[n, to], o_rs.at[n, z], {"expert": to})

    def o_arrival(n, turn):
        source = shift(z, turn, n_z)
        return remote(o_send.at[n, source], o_recv.at[n, source], o_ss.at[n, source], o_rs.at[n, source], {"expert": source})

    def finish_out(n):
        q_copy(n).wait_recv()
        both = q_own[lax.rem(n, 2)] + q_recv[n].astype(f32)
        o_send[n] = both.astype(bf16).reshape(n_z, rows, OUT_COLS)
        for turn in range(1, n_z):
            o_copy(n, turn).start()

    out_chunks = w2.shape[1] // OUT_COLS
    for e in range(experts):
        w2_copy(e).wait()

    def step_out(n, carry):
        columns = pl.ds(pl.multiple_of(n * OUT_COLS, OUT_COLS), OUT_COLS)
        q_send[n] = jnp.dot(wide[0], w2[:, columns], preferred_element_type=f32).astype(bf16)
        q_copy(n).start()
        q_own[lax.rem(n, 2)] = jnp.dot(wide[1], w2[:, columns], preferred_element_type=f32)

        @pl.when(n > 0)
        def _():
            finish_out(n - 1)
        return carry

    lax.fori_loop(0, out_chunks, step_out, 0)
    finish_out(out_chunks - 1)

    for n in range(out_chunks):
        total = o_send[n, z].astype(f32)
        for turn in range(1, n_z):
            o_arrival(n, turn).wait_recv()
        for turn in range(1, n_z):
            total = total + o_recv[n, shift(z, turn, n_z)].astype(f32)
        out[:, n * OUT_COLS:(n + 1) * OUT_COLS] = total.astype(bf16)

    for turn in range(1, blocks):
        route_copy(turn).wait_send()
    for n in range(chunks):
        sib_copy(n).wait_send()
        for turn in range(1, n_z):
            z_copy(n, turn).wait_send()
    for jj in range(per_plane):
        for xx in range(n_x):
            @pl.when(jnp.logical_not(is_me(jj, xx)))
            def _(jj=jj, xx=xx):
                h_copy(jj, xx).wait_send()
    for n in range(out_chunks):
        q_copy(n).wait_send()
        for turn in range(1, n_z):
            o_copy(n, turn).wait_send()


def fused(sizes, xs, route, w1, w2):
    n_z, n_x, top, experts, rows, d_loc, f_loc, span = sizes
    n_dev = 2 * n_z
    chunks, cols = w1.shape[3] // LANE, w2.shape[2]
    slots = top * rows
    out_chunks = cols // OUT_COLS
    bf16, f32 = jnp.bfloat16, jnp.float32
    vmem, dma = pltpu.VMEM, pltpu.SemaphoreType.DMA
    per_plane = n_dev // n_x
    return pl.pallas_call(
        functools.partial(kernel, sizes),
        out_shape=jax.ShapeDtypeStruct((rows, cols), bf16),
        in_specs=[pl.BlockSpec(memory_space=pltpu.VMEM)] * 2 + [pl.BlockSpec(memory_space=pl.ANY)] * 2,
        out_specs=pl.BlockSpec(memory_space=pltpu.VMEM),
        scratch_shapes=[
            vmem((n_dev, rows, LANE), f32),
            vmem((chunks, experts * d_loc, 2 * LANE), bf16),
            vmem((experts * span * LANE, cols), bf16),
            vmem((2, n_z * slots, experts * d_loc), bf16),
            vmem((chunks, n_z * slots, 2 * LANE), bf16),
            vmem((chunks, n_z * slots, 2 * LANE), bf16),
            vmem((2, n_z * slots, 2 * LANE), f32),
            vmem((chunks, n_z, slots, 2 * LANE), bf16),
            vmem((chunks, n_z, slots, 2 * LANE), bf16),
            vmem((chunks, slots, LANE), bf16),
            vmem((n_dev, span, slots, LANE), bf16),
            vmem((2, n_z * rows, experts * span * LANE), bf16),
            vmem((out_chunks, n_z * rows, OUT_COLS), bf16),
            vmem((out_chunks, n_z * rows, OUT_COLS), bf16),
            vmem((2, n_z * rows, OUT_COLS), f32),
            vmem((out_chunks, n_z, rows, OUT_COLS), bf16),
            vmem((out_chunks, n_z, rows, OUT_COLS), bf16),
            dma((chunks, experts, 2)), dma((experts,)),
            dma((n_dev,)), dma((n_dev,)),
            dma((chunks,)), dma((chunks,)),
            dma((chunks, n_z)), dma((chunks, n_z)),
            dma((per_plane, n_x)), dma((n_dev,)),
            dma((out_chunks,)), dma((out_chunks,)),
            dma((out_chunks, n_z)), dma((out_chunks, n_z)),
        ],
        compiler_params=pltpu.CompilerParams(
            collective_id=0, has_side_effects=True, vmem_limit_bytes=58 * 1024 * 1024),
    )(xs, route, w1, w2)


def kernel_sizes(n_z, n_c, n_x, top, experts, rows, d_loc, f_loc, units, cols):
    if n_c != 2 or units % LANE or cols % OUT_COLS or rows % 16 or (n_z * n_c) % n_x:
        return None
    spans = [-(-((j + 1) * f_loc) // LANE) - j * f_loc // LANE for j in range(n_z * n_c // n_x)]
    span = max(spans)
    chunks = units // LANE
    if any(j * f_loc // LANE + span > chunks for j in range(len(spans))):
        return None
    if 2 * n_z * top * rows * experts * d_loc * 2 > 8 * 1024 * 1024:
        return None
    return n_z, n_x, top, experts, rows, d_loc, f_loc, span


def plain(tokens, route, w1, w2, n_x):
    f32, bf16 = jnp.float32, jnp.bfloat16
    n_z, n_c = lax.axis_size("expert"), lax.axis_size("learner")
    c, x = lax.axis_index("learner"), lax.axis_index("replica")
    n_dev = n_z * n_c
    steps, rows_dev, _ = tokens.shape
    experts, d_loc, _, units = w1.shape
    f_loc, cols = w2.shape[1:]
    top = route.shape[2] // 2
    piece = units // n_dev
    n_rows = steps * rows_dev * n_dev
    xs = lax.all_to_all(tokens, ROW_AXES, split_axis=2, concat_axis=1, tiled=True).reshape(n_rows, d_loc)
    route = route.reshape(n_dev, steps, rows_dev, 2 * top).swapaxes(0, 1).reshape(n_rows, 2 * top)
    ids = route[:, :top].T.astype(jnp.int32)
    share = route[:, top:].T
    w1 = w1.reshape(experts * d_loc, 2 * units)
    w2 = w2.reshape(experts * f_loc, cols)
    names = jnp.arange(experts, dtype=jnp.int32)
    picked = ids[:, :, None] == names
    masked = jnp.where(picked[..., None], xs[None, :, None, :], jnp.zeros((), bf16))
    part = jnp.dot(masked.reshape(top * n_rows, experts * d_loc), w1, preferred_element_type=f32)
    part = part.astype(bf16).reshape(top * n_rows, 2, n_z, n_c, piece)

    def core_sum(value, axis):
        mine = lax.dynamic_index_in_dim(value, c, axis, keepdims=False)
        other = lax.dynamic_index_in_dim(value, 1 - c, axis, keepdims=False)
        got = lax.ppermute(other, "learner", [(0, 1), (1, 0)])
        return (mine.astype(f32) + got.astype(f32)).astype(bf16)

    half = jnp.moveaxis(core_sum(part, 3), 2, 0)
    got = lax.all_to_all(half, "expert", split_axis=0, concat_axis=0, tiled=True)
    total = jnp.sum(got.astype(f32), axis=0)
    hidden = jax.nn.silu(total[:, 0]) * total[:, 1]
    hidden = (hidden * share.reshape(-1)[:, None]).astype(bf16)

    pieces = []
    for turn in range(n_x):
        pairs = []
        for zz in range(n_z):
            for xx in range(n_x):
                for cc in range(n_c):
                    q = zz * n_c + cc
                    owner = (n_dev // n_x) * xx + q // n_x
                    source = (zz * n_x + xx) * n_c + cc
                    target = (owner // n_c * n_x + (q + turn) % n_x) * n_c + owner % n_c
                    pairs.append((source, target))
        pieces.append(lax.ppermute(hidden, ("expert", "replica", "learner"), pairs))
    stack = jnp.stack(pieces)
    order = jnp.mod(x - jnp.arange(n_x), n_x)
    ordered = jnp.take(stack, order, axis=0)
    h = jnp.moveaxis(ordered, 0, 1).reshape(top, n_rows, f_loc)
    wide = jnp.zeros((n_rows, experts, f_loc), bf16)
    for k in range(top):
        wide = wide + jnp.where(picked[k][..., None], h[k][:, None, :], jnp.zeros((), bf16))
    out = jnp.dot(wide.reshape(n_rows, experts * f_loc), w2, preferred_element_type=f32)
    out = out.astype(bf16).reshape(steps, n_z, n_c, rows_dev, cols)
    half = jnp.moveaxis(core_sum(out, 2), 1, 0)
    got = lax.all_to_all(half, "expert", split_axis=0, concat_axis=0, tiled=True)
    return jnp.sum(got.astype(f32), axis=0).astype(bf16)


def body(tokens, gates, expert_ids, gate_up_tiles, gate_up_scales, down_tiles, down_scales):
    steps, rows_dev, width = tokens.shape
    top = expert_ids.shape[2]
    n_z = lax.axis_size("expert")
    n_c = lax.axis_size("learner")
    n_x = lax.axis_size("replica")
    n_dev = n_z * n_c
    z, c, x = lax.axis_index("expert"), lax.axis_index("learner"), lax.axis_index("replica")
    me = z * n_c + c
    experts, d_loc, _, units = gate_up_tiles.shape
    f_loc, cols = down_tiles.shape[1:]
    tile = width // gate_up_scales.shape[1]
    f32, bf16 = jnp.float32, jnp.bfloat16

    def take(scales, axis, first, count):
        index = (first + jnp.arange(count)) // tile
        onehot = (index[:, None] == jnp.arange(scales.shape[axis])[None, :]).astype(f32)
        return jnp.moveaxis(
            jnp.tensordot(scales, onehot, axes=([axis], [1]), precision=lax.Precision.HIGHEST), -1, axis
        )

    s1 = take(take(gate_up_scales, 1, me * d_loc, d_loc), 3, x * units, units)
    w1 = (gate_up_tiles.astype(f32) * s1).astype(bf16)
    s2 = take(take(down_scales, 1, me * f_loc, f_loc), 2, x * cols, cols)
    w2 = (down_tiles.astype(f32) * s2).astype(bf16)


    rows = steps * rows_dev
    share = gates / jnp.sum(gates, axis=2, keepdims=True)
    route = jnp.concatenate([expert_ids.astype(f32), share], axis=2).reshape(1, rows, 2 * top)
    sizes = kernel_sizes(n_z, n_c, n_x, top, experts, rows, d_loc, f_loc, units, cols)
    if sizes is None:
        route = lax.all_gather(route, ROW_AXES, axis=0, tiled=True)
        return plain(tokens, route, w1, w2, n_x)
    xs = jnp.swapaxes(tokens.reshape(rows, n_dev, d_loc), 0, 1)
    xs = lax.all_to_all(xs, ROW_AXES, split_axis=0, concat_axis=0, tiled=True)
    route = jnp.pad(route[0], ((0, 0), (0, LANE - 2 * top)))
    out = fused(sizes, xs, route, jnp.swapaxes(w1, 1, 2), w2)
    return out.reshape(steps, rows_dev, cols)


def solution(mesh):
    placed = (
        P(None, ("group", "expert", "learner"), None),
        P(None, ("group", "expert", "learner"), None),
        P(None, ("group", "expert", "learner"), None),
        P(None, ("expert", "learner"), None, "replica"),
        P(),
        P(None, ("expert", "learner"), "replica"),
        P(),
    )
    return jax.shard_map(
        body,
        mesh=mesh,
        in_specs=placed,
        out_specs=P(None, ("group", "expert", "learner"), "replica"),
        check_vma=False,
    )
```

```python
import functools

import jax
import jax.numpy as jnp
from jax import lax
from jax.experimental import pallas as pl
from jax.experimental.pallas import tpu as pltpu
from jax.sharding import PartitionSpec as P

ROW_AXES = ("expert", "learner")
LANE = 128
OUT_COLS = 512


def shift(index, by, count):
    return lax.rem(index + by, count)


def kernel(sizes, xs, my_route, w1_in, w2_in, out, route, w1, w2, xm, s_send, s_recv, own, z_send, z_recv, z_pass, hid, h_recv,
           wide, q_send, q_recv, q_own, o_send, o_recv, o_pass,
           w1_s, w2_s, r_ss, r_rs, s_ss, s_rs, z_ss, z_rs, z_ps, h_ss, h_rs, q_ss, q_rs, o_ss, o_rs, o_ps):
    n_z, n_x, top, experts, rows, d_loc, f_loc, span = sizes
    n_c = 2
    f32, bf16 = jnp.float32, jnp.bfloat16
    z, c, x = lax.axis_index("expert"), lax.axis_index("learner"), lax.axis_index("replica")
    me = z * n_c + c
    chunks = w1.shape[0]
    slots = top * rows
    per_plane = n_z * n_c // n_x
    sibling = {"learner": 1 - c}

    def remote(src, dst, send, recv, device):
        return pltpu.make_async_remote_copy(
            src_ref=src, dst_ref=dst, send_sem=send, recv_sem=recv,
            device_id=device, device_id_type=pl.DeviceIdType.MESH)

    depth = span * LANE

    def w1_copy(n, e, g):
        return pltpu.make_async_copy(
            w1_in.at[e, g, :, pl.ds(pl.multiple_of(n * LANE, LANE), LANE)],
            w1.at[n, pl.ds(e * d_loc, d_loc), pl.ds(g * LANE, LANE)], w1_s.at[n, e, g])

    offset = lax.rem(lax.rem(me, per_plane) * f_loc, LANE)

    def w2_copy(e):
        return pltpu.make_async_copy(
            w2_in.at[e], w2.at[pl.ds(pl.multiple_of(e * depth + offset, 16), f_loc)], w2_s.at[e])

    for n in range(chunks):
        for e in range(experts):
            for g in range(2):
                w1_copy(n, e, g).start()
    for e in range(experts):
        w2_copy(e).start()

    barrier = pltpu.get_barrier_semaphore()
    everyone = n_z * n_c * n_x
    here = (z * n_x + x) * n_c + c
    for turn in range(1, everyone):
        there = shift(here, turn, everyone)
        pl.semaphore_signal(
            barrier, inc=1,
            device_id={"expert": there // (n_x * n_c), "replica": there // n_c % n_x, "learner": there % n_c},
            device_id_type=pl.DeviceIdType.MESH)

    def block_of(half, zz):
        return zz * n_c + (c if half else 1 - c)

    pl.semaphore_wait(barrier, everyone - 1)
    blocks = n_z * n_c

    def route_copy(turn):
        to = shift(me, turn, blocks)
        return remote(my_route, route.at[me], r_ss.at[to], r_rs.at[me],
                      {"expert": to // n_c, "learner": to % n_c})

    def route_arrival(turn):
        source = shift(me, turn, blocks)
        return remote(my_route, route.at[source], r_ss.at[source], r_rs.at[source],
                      {"expert": source // n_c, "learner": source % n_c})

    for turn in range(1, blocks):
        route_copy(turn).start()
    route[me] = my_route[...]
    if depth > f_loc:
        gap = depth - f_loc
        for option in sorted({j * f_loc % LANE for j in range(per_plane)}):
            @pl.when(offset == option)
            def _(option=option):
                for e in range(experts):
                    if option:
                        w2[e * depth:e * depth + option] = jnp.zeros((option, w2.shape[1]), bf16)
                    if gap > option:
                        w2[e * depth + option + f_loc:(e + 1) * depth] = jnp.zeros((gap - option, w2.shape[1]), bf16)
    for turn in range(1, blocks):
        route_arrival(turn).wait_recv()

    for half in range(2):
        for zz in range(n_z):
            p = block_of(half, zz)
            ids = route[p]
            value = xs[p]
            for k in range(top):
                name = jnp.broadcast_to(ids[:, k:k + 1], (rows, d_loc))
                for e in range(experts):
                    xm[half, zz * slots + k * rows:zz * slots + (k + 1) * rows, e * d_loc:(e + 1) * d_loc] = (
                        jnp.where(name == e, value.astype(f32), 0.0).astype(bf16))

    near = z + 1 - 2 * lax.rem(z, 2)
    far_mid = jnp.where(z < 2, 2, 1)
    far_end = jnp.where(z < 2, 3, 0)
    at_end = (z == 0) | (z == n_z - 1)

    def line(send, recv, relay, own, ss, rs, ps):
        def direct(n, block, slot):
            return remote(send.at[n, block], recv.at[n, slot], ss.at[n, block], rs.at[n, slot], {"expert": block})

        def hand(n, block, slot):
            return remote(send.at[n, block], relay.at[n, slot], ss.at[n, block], ps.at[n, slot], {"expert": near})

        def begin(n):
            @pl.when(at_end)
            def _():
                for slot, block in ((1, far_end), (0, far_mid)):
                    send[n, block] = own[n, block].astype(bf16)
                    hand(n, block, slot).start()
            send[n, near] = own[n, near].astype(bf16)
            direct(n, near, 0).start()

        def pass_on(n):
            @pl.when(jnp.logical_not(at_end))
            def _():
                for slot, block in ((1, far_end), (0, far_mid)):
                    hand(n, block, slot).wait_recv()
                    send[n, block] = (own[n, block] + relay[n, slot].astype(f32)).astype(bf16)
                    direct(n, block, 1).start()

        def total(n):
            direct(n, near, 0).wait_recv()
            direct(n, far_mid, 1).wait_recv()
            return own[n, z] + recv[n, 0].astype(f32) + recv[n, 1].astype(f32)

        def close(n):
            for block in (near, far_mid, far_end):
                direct(n, block, 0).wait_send()

        return begin, pass_on, total, close

    def sib_copy(n):
        return remote(s_send.at[n], s_recv.at[n], s_ss.at[n], s_rs.at[n], sibling)

    begin, pass_on, total_of, close = line(z_send, z_recv, z_pass, own, z_ss, z_rs, z_ps)

    def finish(n):
        sib_copy(n).wait_recv()
        own[n] += s_recv[n].astype(f32).reshape(n_z, slots, 2 * LANE)
        begin(n)

    def step(n, carry):
        for e in range(experts):
            for g in range(2):
                w1_copy(n, e, g).wait()
        s_send[n] = jnp.dot(xm[0], w1[n], preferred_element_type=f32).astype(bf16)
        sib_copy(n).start()
        own[n] = jnp.dot(xm[1], w1[n], preferred_element_type=f32).reshape(n_z, slots, 2 * LANE)

        @pl.when(n > 0)
        def _():
            finish(n - 1)

        @pl.when(n > 1)
        def _():
            pass_on(n - 2)
        return carry

    lax.fori_loop(0, chunks, step, 0)
    finish(chunks - 1)
    for n in range(max(chunks - 2, 0), chunks):
        pass_on(n)

    mine = route[me]

    def h_copy(jj, xx):
        owner = per_plane * x + jj
        first = jj * f_loc // LANE
        return remote(hid.at[pl.ds(first, span)], h_recv.at[me], h_ss.at[jj, xx], h_rs.at[me],
                      {"expert": owner // n_c, "learner": owner % n_c, "replica": xx})

    def is_me(jj, xx):
        return (per_plane * x + jj == me) & (x == xx)

    for n in range(chunks):
        total = total_of(n)
        gate, up = total[:, :LANE], total[:, LANE:]
        value = gate / (1.0 + jnp.exp(-gate)) * up
        for k in range(top):
            part = value[k * rows:(k + 1) * rows] * mine[:, top + k:top + k + 1]
            hid[n, k * rows:(k + 1) * rows, :] = part.astype(bf16)
        for jj in range(per_plane):
            first = jj * f_loc // LANE
            if first + span - 1 != n:
                continue
            for xx in range(n_x):
                @pl.when(jnp.logical_not(is_me(jj, xx)))
                def _(jj=jj, xx=xx):
                    h_copy(jj, xx).start()

                @pl.when(is_me(jj, xx))
                def _(first=first):
                    h_recv[me] = hid[first:first + span]

    source_x = me // per_plane
    for p in range(n_z * n_c):
        @pl.when(jnp.logical_not((p == me) & (source_x == x)))
        def _(p=p):
            remote(hid.at[pl.ds(0, span)], h_recv.at[p], h_ss.at[0, 0], h_rs.at[p],
                   {"expert": p // n_c, "learner": p % n_c, "replica": source_x}).wait_recv()

    for half in range(2):
        for zz in range(n_z):
            p = block_of(half, zz)
            ids = route[p]
            for e in range(experts):
                for s in range(span):
                    value = jnp.zeros((rows, LANE), f32)
                    for k in range(top):
                        name = jnp.broadcast_to(ids[:, k:k + 1], (rows, LANE))
                        value = value + jnp.where(name == e, h_recv[p, s, k * rows:(k + 1) * rows, :].astype(f32), 0.0)
                    wide[half, zz * rows:(zz + 1) * rows, e * depth + s * LANE:e * depth + (s + 1) * LANE] = value.astype(bf16)

    def q_copy(n):
        return remote(q_send.at[n], q_recv.at[n], q_ss.at[n], q_rs.at[n], sibling)

    begin_out, pass_out, total_out, close_out = line(o_send, o_recv, o_pass, q_own, o_ss, o_rs, o_ps)

    def finish_out(n):
        q_copy(n).wait_recv()
        q_own[n] += q_recv[n].astype(f32).reshape(n_z, rows, OUT_COLS)
        begin_out(n)

    out_chunks = w2.shape[1] // OUT_COLS
    for e in range(experts):
        w2_copy(e).wait()

    def step_out(n, carry):
        columns = pl.ds(pl.multiple_of(n * OUT_COLS, OUT_COLS), OUT_COLS)
        q_send[n] = jnp.dot(wide[0], w2[:, columns], preferred_element_type=f32).astype(bf16)
        q_copy(n).start()
        q_own[n] = jnp.dot(wide[1], w2[:, columns], preferred_element_type=f32).reshape(n_z, rows, OUT_COLS)

        @pl.when(n > 0)
        def _():
            finish_out(n - 1)

        @pl.when(n > 1)
        def _():
            pass_out(n - 2)
        return carry

    lax.fori_loop(0, out_chunks, step_out, 0)
    finish_out(out_chunks - 1)
    for n in range(max(out_chunks - 2, 0), out_chunks):
        pass_out(n)

    for n in range(out_chunks):
        out[:, n * OUT_COLS:(n + 1) * OUT_COLS] = total_out(n).astype(bf16)

    for turn in range(1, blocks):
        route_copy(turn).wait_send()
    for n in range(chunks):
        sib_copy(n).wait_send()
        close(n)
    for jj in range(per_plane):
        for xx in range(n_x):
            @pl.when(jnp.logical_not(is_me(jj, xx)))
            def _(jj=jj, xx=xx):
                h_copy(jj, xx).wait_send()
    for n in range(out_chunks):
        q_copy(n).wait_send()
        close_out(n)


def fused(sizes, xs, route, w1, w2):
    n_z, n_x, top, experts, rows, d_loc, f_loc, span = sizes
    n_dev = 2 * n_z
    chunks, cols = w1.shape[3] // LANE, w2.shape[2]
    slots = top * rows
    out_chunks = cols // OUT_COLS
    bf16, f32 = jnp.bfloat16, jnp.float32
    vmem, dma = pltpu.VMEM, pltpu.SemaphoreType.DMA
    per_plane = n_dev // n_x
    return pl.pallas_call(
        functools.partial(kernel, sizes),
        out_shape=jax.ShapeDtypeStruct((rows, cols), bf16),
        in_specs=[pl.BlockSpec(memory_space=pltpu.VMEM)] * 2 + [pl.BlockSpec(memory_space=pl.ANY)] * 2,
        out_specs=pl.BlockSpec(memory_space=pltpu.VMEM),
        scratch_shapes=[
            vmem((n_dev, rows, LANE), f32),
            vmem((chunks, experts * d_loc, 2 * LANE), bf16),
            vmem((experts * span * LANE, cols), bf16),
            vmem((2, n_z * slots, experts * d_loc), bf16),
            vmem((chunks, n_z * slots, 2 * LANE), bf16),
            vmem((chunks, n_z * slots, 2 * LANE), bf16),
            vmem((chunks, n_z, slots, 2 * LANE), f32),
            vmem((chunks, n_z, slots, 2 * LANE), bf16),
            vmem((chunks, 2, slots, 2 * LANE), bf16),
            vmem((chunks, 2, slots, 2 * LANE), bf16),
            vmem((chunks, slots, LANE), bf16),
            vmem((n_dev, span, slots, LANE), bf16),
            vmem((2, n_z * rows, experts * span * LANE), bf16),
            vmem((out_chunks, n_z * rows, OUT_COLS), bf16),
            vmem((out_chunks, n_z * rows, OUT_COLS), bf16),
            vmem((out_chunks, n_z, rows, OUT_COLS), f32),
            vmem((out_chunks, n_z, rows, OUT_COLS), bf16),
            vmem((out_chunks, 2, rows, OUT_COLS), bf16),
            vmem((out_chunks, 2, rows, OUT_COLS), bf16),
            dma((chunks, experts, 2)), dma((experts,)),
            dma((n_dev,)), dma((n_dev,)),
            dma((chunks,)), dma((chunks,)),
            dma((chunks, n_z)), dma((chunks, 2)), dma((chunks, 2)),
            dma((per_plane, n_x)), dma((n_dev,)),
            dma((out_chunks,)), dma((out_chunks,)),
            dma((out_chunks, n_z)), dma((out_chunks, 2)), dma((out_chunks, 2)),
        ],
        compiler_params=pltpu.CompilerParams(
            collective_id=0, has_side_effects=True, vmem_limit_bytes=58 * 1024 * 1024),
    )(xs, route, w1, w2)


def kernel_sizes(n_z, n_c, n_x, top, experts, rows, d_loc, f_loc, units, cols):
    if n_z != 4 or n_c != 2 or units % LANE or cols % OUT_COLS or rows % 16 or (n_z * n_c) % n_x:
        return None
    spans = [-(-((j + 1) * f_loc) // LANE) - j * f_loc // LANE for j in range(n_z * n_c // n_x)]
    span = max(spans)
    chunks = units // LANE
    if any(j * f_loc // LANE + span > chunks for j in range(len(spans))):
        return None
    if 2 * n_z * top * rows * experts * d_loc * 2 > 8 * 1024 * 1024:
        return None
    return n_z, n_x, top, experts, rows, d_loc, f_loc, span


def plain(tokens, route, w1, w2, n_x):
    f32, bf16 = jnp.float32, jnp.bfloat16
    n_z, n_c = lax.axis_size("expert"), lax.axis_size("learner")
    c, x = lax.axis_index("learner"), lax.axis_index("replica")
    n_dev = n_z * n_c
    steps, rows_dev, _ = tokens.shape
    experts, d_loc, _, units = w1.shape
    f_loc, cols = w2.shape[1:]
    top = route.shape[2] // 2
    piece = units // n_dev
    n_rows = steps * rows_dev * n_dev
    xs = lax.all_to_all(tokens, ROW_AXES, split_axis=2, concat_axis=1, tiled=True).reshape(n_rows, d_loc)
    route = route.reshape(n_dev, steps, rows_dev, 2 * top).swapaxes(0, 1).reshape(n_rows, 2 * top)
    ids = route[:, :top].T.astype(jnp.int32)
    share = route[:, top:].T
    w1 = w1.reshape(experts * d_loc, 2 * units)
    w2 = w2.reshape(experts * f_loc, cols)
    names = jnp.arange(experts, dtype=jnp.int32)
    picked = ids[:, :, None] == names
    masked = jnp.where(picked[..., None], xs[None, :, None, :], jnp.zeros((), bf16))
    part = jnp.dot(masked.reshape(top * n_rows, experts * d_loc), w1, preferred_element_type=f32)
    part = part.astype(bf16).reshape(top * n_rows, 2, n_z, n_c, piece)

    def core_sum(value, axis):
        mine = lax.dynamic_index_in_dim(value, c, axis, keepdims=False)
        other = lax.dynamic_index_in_dim(value, 1 - c, axis, keepdims=False)
        got = lax.ppermute(other, "learner", [(0, 1), (1, 0)])
        return (mine.astype(f32) + got.astype(f32)).astype(bf16)

    half = jnp.moveaxis(core_sum(part, 3), 2, 0)
    got = lax.all_to_all(half, "expert", split_axis=0, concat_axis=0, tiled=True)
    total = jnp.sum(got.astype(f32), axis=0)
    hidden = jax.nn.silu(total[:, 0]) * total[:, 1]
    hidden = (hidden * share.reshape(-1)[:, None]).astype(bf16)

    pieces = []
    for turn in range(n_x):
        pairs = []
        for zz in range(n_z):
            for xx in range(n_x):
                for cc in range(n_c):
                    q = zz * n_c + cc
                    owner = (n_dev // n_x) * xx + q // n_x
                    source = (zz * n_x + xx) * n_c + cc
                    target = (owner // n_c * n_x + (q + turn) % n_x) * n_c + owner % n_c
                    pairs.append((source, target))
        pieces.append(lax.ppermute(hidden, ("expert", "replica", "learner"), pairs))
    stack = jnp.stack(pieces)
    order = jnp.mod(x - jnp.arange(n_x), n_x)
    ordered = jnp.take(stack, order, axis=0)
    h = jnp.moveaxis(ordered, 0, 1).reshape(top, n_rows, f_loc)
    wide = jnp.zeros((n_rows, experts, f_loc), bf16)
    for k in range(top):
        wide = wide + jnp.where(picked[k][..., None], h[k][:, None, :], jnp.zeros((), bf16))
    out = jnp.dot(wide.reshape(n_rows, experts * f_loc), w2, preferred_element_type=f32)
    out = out.astype(bf16).reshape(steps, n_z, n_c, rows_dev, cols)
    half = jnp.moveaxis(core_sum(out, 2), 1, 0)
    got = lax.all_to_all(half, "expert", split_axis=0, concat_axis=0, tiled=True)
    return jnp.sum(got.astype(f32), axis=0).astype(bf16)


def body(tokens, gates, expert_ids, gate_up_tiles, gate_up_scales, down_tiles, down_scales):
    steps, rows_dev, width = tokens.shape
    top = expert_ids.shape[2]
    n_z = lax.axis_size("expert")
    n_c = lax.axis_size("learner")
    n_x = lax.axis_size("replica")
    n_dev = n_z * n_c
    z, c, x = lax.axis_index("expert"), lax.axis_index("learner"), lax.axis_index("replica")
    me = z * n_c + c
    experts, d_loc, _, units = gate_up_tiles.shape
    f_loc, cols = down_tiles.shape[1:]
    tile = width // gate_up_scales.shape[1]
    f32, bf16 = jnp.float32, jnp.bfloat16

    def take(scales, axis, first, count):
        index = (first + jnp.arange(count)) // tile
        onehot = (index[:, None] == jnp.arange(scales.shape[axis])[None, :]).astype(f32)
        return jnp.moveaxis(
            jnp.tensordot(scales, onehot, axes=([axis], [1]), precision=lax.Precision.HIGHEST), -1, axis
        )

    s1 = take(take(gate_up_scales, 1, me * d_loc, d_loc), 3, x * units, units)
    w1 = (gate_up_tiles.astype(f32) * s1).astype(bf16)
    s2 = take(take(down_scales, 1, me * f_loc, f_loc), 2, x * cols, cols)
    w2 = (down_tiles.astype(f32) * s2).astype(bf16)


    rows = steps * rows_dev
    share = gates / jnp.sum(gates, axis=2, keepdims=True)
    route = jnp.concatenate([expert_ids.astype(f32), share], axis=2).reshape(1, rows, 2 * top)
    sizes = kernel_sizes(n_z, n_c, n_x, top, experts, rows, d_loc, f_loc, units, cols)
    if sizes is None:
        route = lax.all_gather(route, ROW_AXES, axis=0, tiled=True)
        return plain(tokens, route, w1, w2, n_x)
    xs = jnp.swapaxes(tokens.reshape(rows, n_dev, d_loc), 0, 1)
    xs = lax.all_to_all(xs, ROW_AXES, split_axis=0, concat_axis=0, tiled=True)
    route = jnp.pad(route[0], ((0, 0), (0, LANE - 2 * top)))
    out = fused(sizes, xs, route, jnp.swapaxes(w1, 1, 2), w2)
    return out.reshape(steps, rows_dev, cols)


def solution(mesh):
    placed = (
        P(None, ("group", "expert", "learner"), None),
        P(None, ("group", "expert", "learner"), None),
        P(None, ("group", "expert", "learner"), None),
        P(None, ("expert", "learner"), None, "replica"),
        P(),
        P(None, ("expert", "learner"), "replica"),
        P(),
    )
    return jax.shard_map(
        body,
        mesh=mesh,
        in_specs=placed,
        out_specs=P(None, ("group", "expert", "learner"), "replica"),
        check_vma=False,
    )
```

```python
import functools

import jax
import jax.numpy as jnp
from jax import lax
from jax.experimental import pallas as pl
from jax.experimental.pallas import tpu as pltpu
from jax.sharding import PartitionSpec as P

ROW_AXES = ("expert", "learner")
LANE = 128
OUT_COLS = 512


def shift(index, by, count):
    return lax.rem(index + by, count)


def kernel(sizes, xs, my_route, s2, w1_in, w2_in, out, route, w1, w2, xm, s_send, s_recv, own, z_send, z_recv, z_pass, hid, h_recv,
           wide, q_send, q_recv, q_own, o_send, o_recv, o_pass,
           w1_s, w2_s, r_ss, r_rs, s_ss, s_rs, z_ss, z_rs, z_ps, h_ss, h_fs, h_rs, q_ss, q_rs, o_ss, o_rs, o_ps):
    n_z, n_x, top, experts, rows, d_loc, f_loc, span = sizes
    n_c = 2
    f32, bf16 = jnp.float32, jnp.bfloat16
    z, c, x = lax.axis_index("expert"), lax.axis_index("learner"), lax.axis_index("replica")
    me = z * n_c + c
    chunks = w1.shape[0]
    slots = top * rows
    per_plane = n_z * n_c // n_x
    sibling = {"learner": 1 - c}

    def remote(src, dst, send, recv, device):
        return pltpu.make_async_remote_copy(
            src_ref=src, dst_ref=dst, send_sem=send, recv_sem=recv,
            device_id=device, device_id_type=pl.DeviceIdType.MESH)

    depth = span * LANE

    def w1_copy(n, e, g):
        return pltpu.make_async_copy(
            w1_in.at[e, g, :, pl.ds(pl.multiple_of(n * LANE, LANE), LANE)],
            w1.at[n, pl.ds(e * d_loc, d_loc), pl.ds(g * LANE, LANE)], w1_s.at[n, e, g])

    offset = lax.rem(lax.rem(me, per_plane) * f_loc, LANE)

    def w2_copy(e):
        return pltpu.make_async_copy(
            w2_in.at[e], w2.at[pl.ds(pl.multiple_of(e * depth + offset, 16), f_loc)], w2_s.at[e])

    for n in range(chunks):
        for e in range(experts):
            for g in range(2):
                w1_copy(n, e, g).start()
    for e in range(experts):
        w2_copy(e).start()

    barrier = pltpu.get_barrier_semaphore()
    everyone = n_z * n_c * n_x
    here = (z * n_x + x) * n_c + c
    for turn in range(1, everyone):
        there = shift(here, turn, everyone)
        pl.semaphore_signal(
            barrier, inc=1,
            device_id={"expert": there // (n_x * n_c), "replica": there // n_c % n_x, "learner": there % n_c},
            device_id_type=pl.DeviceIdType.MESH)

    def block_of(half, zz):
        return zz * n_c + (c if half else 1 - c)

    pl.semaphore_wait(barrier, everyone - 1)
    blocks = n_z * n_c

    def route_copy(turn):
        to = shift(me, turn, blocks)
        return remote(my_route, route.at[me], r_ss.at[to], r_rs.at[me],
                      {"expert": to // n_c, "learner": to % n_c})

    def route_arrival(turn):
        source = shift(me, turn, blocks)
        return remote(my_route, route.at[source], r_ss.at[source], r_rs.at[source],
                      {"expert": source // n_c, "learner": source % n_c})

    for turn in range(1, blocks):
        route_copy(turn).start()
    route[me] = my_route[...]
    if depth > f_loc:
        gap = depth - f_loc
        for option in sorted({j * f_loc % LANE for j in range(per_plane)}):
            @pl.when(offset == option)
            def _(option=option):
                for e in range(experts):
                    if option:
                        w2[e * depth:e * depth + option] = jnp.zeros((option, w2.shape[1]), bf16)
                    if gap > option:
                        w2[e * depth + option + f_loc:(e + 1) * depth] = jnp.zeros((gap - option, w2.shape[1]), bf16)
    for turn in range(1, blocks):
        route_arrival(turn).wait_recv()

    for half in range(2):
        for zz in range(n_z):
            p = block_of(half, zz)
            ids = route[p]
            value = xs[p]
            for k in range(top):
                name = jnp.broadcast_to(ids[:, k:k + 1], (rows, d_loc))
                for e in range(experts):
                    xm[half, zz * slots + k * rows:zz * slots + (k + 1) * rows, e * d_loc:(e + 1) * d_loc] = (
                        jnp.where(name == e, value.astype(f32), 0.0).astype(bf16))

    near = z + 1 - 2 * lax.rem(z, 2)
    far_mid = jnp.where(z < 2, 2, 1)
    far_end = jnp.where(z < 2, 3, 0)
    at_end = (z == 0) | (z == n_z - 1)

    def line(send, recv, relay, own, ss, rs, ps):
        def direct(n, block, slot):
            return remote(send.at[n, block], recv.at[n, slot], ss.at[n, block], rs.at[n, slot], {"expert": block})

        def hand(n, block, slot):
            return remote(send.at[n, block], relay.at[n, slot], ss.at[n, block], ps.at[n, slot], {"expert": near})

        def begin(n):
            @pl.when(at_end)
            def _():
                for slot, block in ((1, far_end), (0, far_mid)):
                    send[n, block] = own[n, block].astype(bf16)
                    hand(n, block, slot).start()
            send[n, near] = own[n, near].astype(bf16)
            direct(n, near, 0).start()

        def pass_on(n):
            @pl.when(jnp.logical_not(at_end))
            def _():
                for slot, block in ((1, far_end), (0, far_mid)):
                    hand(n, block, slot).wait_recv()
                    send[n, block] = (own[n, block] + relay[n, slot].astype(f32)).astype(bf16)
                    direct(n, block, 1).start()

        def total(n):
            direct(n, near, 0).wait_recv()
            direct(n, far_mid, 1).wait_recv()
            return own[n, z] + recv[n, 0].astype(f32) + recv[n, 1].astype(f32)

        def close(n):
            for block in (near, far_mid, far_end):
                direct(n, block, 0).wait_send()

        return begin, pass_on, total, close

    def sib_copy(n):
        return remote(s_send.at[n], s_recv.at[n], s_ss.at[n], s_rs.at[n], sibling)

    begin, pass_on, total_of, close = line(z_send, z_recv, z_pass, own, z_ss, z_rs, z_ps)

    def finish(n):
        sib_copy(n).wait_recv()
        own[n] += s_recv[n].astype(f32).reshape(n_z, slots, 2 * LANE)
        begin(n)

    def scale_down(e):
        w2_copy(e).wait()
        band = pl.ds(pl.multiple_of(e * depth + offset, 16), f_loc)
        scales = s2[e]
        for b in range(w2.shape[1] // LANE):
            columns = slice(b * LANE, (b + 1) * LANE)
            w2[band, columns] = (w2[band, columns].astype(f32) * scales[:, b:b + 1]).astype(bf16)

    def step(n, carry):
        for e in range(experts):
            for g in range(2):
                w1_copy(n, e, g).wait()
        s_send[n] = jnp.dot(xm[0], w1[n], preferred_element_type=f32).astype(bf16)
        sib_copy(n).start()
        own[n] = jnp.dot(xm[1], w1[n], preferred_element_type=f32).reshape(n_z, slots, 2 * LANE)

        @pl.when(n > 0)
        def _():
            finish(n - 1)

        @pl.when(n > 1)
        def _():
            pass_on(n - 2)

        @pl.when(n < experts)
        def _():
            scale_down(n)
        return carry

    lax.fori_loop(0, chunks, step, 0)
    finish(chunks - 1)
    for n in range(max(chunks - 2, 0), chunks):
        pass_on(n)

    mine = route[me]

    source_x = me // per_plane

    def h_copy(jj):
        owner = per_plane * x + jj
        first = jj * f_loc // LANE
        return remote(hid.at[pl.ds(first, span)], h_recv.at[me], h_ss.at[jj], h_rs.at[me],
                      {"expert": owner // n_c, "learner": owner % n_c})

    def h_forward(p):
        return remote(h_recv.at[p], h_recv.at[p], h_fs.at[p], h_rs.at[p], {"replica": 1 - x})

    def is_me(jj):
        return per_plane * x + jj == me

    for n in range(chunks):
        total = total_of(n)
        gate, up = total[:, :LANE], total[:, LANE:]
        value = gate / (1.0 + jnp.exp(-gate)) * up
        for k in range(top):
            part = value[k * rows:(k + 1) * rows] * mine[:, top + k:top + k + 1]
            hid[n, k * rows:(k + 1) * rows, :] = part.astype(bf16)
        for jj in range(per_plane):
            first = jj * f_loc // LANE
            if first + span - 1 != n:
                continue
            @pl.when(jnp.logical_not(is_me(jj)))
            def _(jj=jj):
                h_copy(jj).start()

            @pl.when(is_me(jj))
            def _(first=first):
                h_recv[me] = hid[first:first + span]

    @pl.when(source_x == x)
    def _():
        h_forward(me).start()
        for turn in range(1, blocks):
            p = shift(me, turn, blocks)
            h_forward(p).wait_recv()
            h_forward(p).start()

    @pl.when(source_x != x)
    def _():
        for p in range(blocks):
            h_forward(p).wait_recv()

    for half in range(2):
        for zz in range(n_z):
            p = block_of(half, zz)
            ids = route[p]
            for e in range(experts):
                for s in range(span):
                    value = jnp.zeros((rows, LANE), f32)
                    for k in range(top):
                        name = jnp.broadcast_to(ids[:, k:k + 1], (rows, LANE))
                        value = value + jnp.where(name == e, h_recv[p, s, k * rows:(k + 1) * rows, :].astype(f32), 0.0)
                    wide[half, zz * rows:(zz + 1) * rows, e * depth + s * LANE:e * depth + (s + 1) * LANE] = value.astype(bf16)

    def q_copy(n):
        return remote(q_send.at[n], q_recv.at[n], q_ss.at[n], q_rs.at[n], sibling)

    begin_out, pass_out, total_out, close_out = line(o_send, o_recv, o_pass, q_own, o_ss, o_rs, o_ps)

    def finish_out(n):
        q_copy(n).wait_recv()
        q_own[n] += q_recv[n].astype(f32).reshape(n_z, rows, OUT_COLS)
        begin_out(n)

    out_chunks = w2.shape[1] // OUT_COLS
    for e in range(chunks, experts):
        scale_down(e)

    def step_out(n, carry):
        columns = pl.ds(pl.multiple_of(n * OUT_COLS, OUT_COLS), OUT_COLS)
        q_send[n] = jnp.dot(wide[0], w2[:, columns], preferred_element_type=f32).astype(bf16)
        q_copy(n).start()
        q_own[n] = jnp.dot(wide[1], w2[:, columns], preferred_element_type=f32).reshape(n_z, rows, OUT_COLS)

        @pl.when(n > 0)
        def _():
            finish_out(n - 1)

        @pl.when(n > 1)
        def _():
            pass_out(n - 2)
        return carry

    lax.fori_loop(0, out_chunks, step_out, 0)
    finish_out(out_chunks - 1)
    for n in range(max(out_chunks - 2, 0), out_chunks):
        pass_out(n)

    for n in range(out_chunks):
        out[:, n * OUT_COLS:(n + 1) * OUT_COLS] = total_out(n).astype(bf16)

    for turn in range(1, blocks):
        route_copy(turn).wait_send()
    for n in range(chunks):
        sib_copy(n).wait_send()
        close(n)
    for jj in range(per_plane):
        @pl.when(jnp.logical_not(is_me(jj)))
        def _(jj=jj):
            h_copy(jj).wait_send()

    @pl.when(source_x == x)
    def _():
        for p in range(blocks):
            h_forward(p).wait_send()
    for n in range(out_chunks):
        q_copy(n).wait_send()
        close_out(n)


def fused(sizes, xs, route, s2, w1, w2):
    n_z, n_x, top, experts, rows, d_loc, f_loc, span = sizes
    n_dev = 2 * n_z
    chunks, cols = w1.shape[3] // LANE, w2.shape[2]
    slots = top * rows
    out_chunks = cols // OUT_COLS
    bf16, f32 = jnp.bfloat16, jnp.float32
    vmem, dma = pltpu.VMEM, pltpu.SemaphoreType.DMA
    per_plane = n_dev // n_x
    return pl.pallas_call(
        functools.partial(kernel, sizes),
        out_shape=jax.ShapeDtypeStruct((rows, cols), bf16),
        in_specs=[pl.BlockSpec(memory_space=pltpu.VMEM)] * 3 + [pl.BlockSpec(memory_space=pl.ANY)] * 2,
        out_specs=pl.BlockSpec(memory_space=pltpu.VMEM),
        scratch_shapes=[
            vmem((n_dev, rows, LANE), f32),
            vmem((chunks, experts * d_loc, 2 * LANE), bf16),
            vmem((experts * span * LANE, cols), bf16),
            vmem((2, n_z * slots, experts * d_loc), bf16),
            vmem((chunks, n_z * slots, 2 * LANE), bf16),
            vmem((chunks, n_z * slots, 2 * LANE), bf16),
            vmem((chunks, n_z, slots, 2 * LANE), f32),
            vmem((chunks, n_z, slots, 2 * LANE), bf16),
            vmem((chunks, 2, slots, 2 * LANE), bf16),
            vmem((chunks, 2, slots, 2 * LANE), bf16),
            vmem((chunks, slots, LANE), bf16),
            vmem((n_dev, span, slots, LANE), bf16),
            vmem((2, n_z * rows, experts * span * LANE), bf16),
            vmem((out_chunks, n_z * rows, OUT_COLS), bf16),
            vmem((out_chunks, n_z * rows, OUT_COLS), bf16),
            vmem((out_chunks, n_z, rows, OUT_COLS), f32),
            vmem((out_chunks, n_z, rows, OUT_COLS), bf16),
            vmem((out_chunks, 2, rows, OUT_COLS), bf16),
            vmem((out_chunks, 2, rows, OUT_COLS), bf16),
            dma((chunks, experts, 2)), dma((experts,)),
            dma((n_dev,)), dma((n_dev,)),
            dma((chunks,)), dma((chunks,)),
            dma((chunks, n_z)), dma((chunks, 2)), dma((chunks, 2)),
            dma((per_plane,)), dma((n_dev,)), dma((n_dev,)),
            dma((out_chunks,)), dma((out_chunks,)),
            dma((out_chunks, n_z)), dma((out_chunks, 2)), dma((out_chunks, 2)),
        ],
        compiler_params=pltpu.CompilerParams(
            collective_id=0, has_side_effects=True, vmem_limit_bytes=58 * 1024 * 1024),
    )(xs, route, s2, w1, w2)


def kernel_sizes(n_z, n_c, n_x, top, experts, rows, d_loc, f_loc, units, cols):
    if n_x != 2 or n_z != 4 or n_c != 2 or units % LANE or cols % OUT_COLS or rows % 16 or (n_z * n_c) % n_x:
        return None
    spans = [-(-((j + 1) * f_loc) // LANE) - j * f_loc // LANE for j in range(n_z * n_c // n_x)]
    span = max(spans)
    chunks = units // LANE
    if any(j * f_loc // LANE + span > chunks for j in range(len(spans))):
        return None
    if 2 * n_z * top * rows * experts * d_loc * 2 > 8 * 1024 * 1024:
        return None
    return n_z, n_x, top, experts, rows, d_loc, f_loc, span


def plain(tokens, route, w1, w2, n_x):
    f32, bf16 = jnp.float32, jnp.bfloat16
    n_z, n_c = lax.axis_size("expert"), lax.axis_size("learner")
    c, x = lax.axis_index("learner"), lax.axis_index("replica")
    n_dev = n_z * n_c
    steps, rows_dev, _ = tokens.shape
    experts, d_loc, _, units = w1.shape
    f_loc, cols = w2.shape[1:]
    top = route.shape[2] // 2
    piece = units // n_dev
    n_rows = steps * rows_dev * n_dev
    xs = lax.all_to_all(tokens, ROW_AXES, split_axis=2, concat_axis=1, tiled=True).reshape(n_rows, d_loc)
    route = route.reshape(n_dev, steps, rows_dev, 2 * top).swapaxes(0, 1).reshape(n_rows, 2 * top)
    ids = route[:, :top].T.astype(jnp.int32)
    share = route[:, top:].T
    w1 = w1.reshape(experts * d_loc, 2 * units)
    w2 = w2.reshape(experts * f_loc, cols)
    names = jnp.arange(experts, dtype=jnp.int32)
    picked = ids[:, :, None] == names
    masked = jnp.where(picked[..., None], xs[None, :, None, :], jnp.zeros((), bf16))
    part = jnp.dot(masked.reshape(top * n_rows, experts * d_loc), w1, preferred_element_type=f32)
    part = part.astype(bf16).reshape(top * n_rows, 2, n_z, n_c, piece)

    def core_sum(value, axis):
        mine = lax.dynamic_index_in_dim(value, c, axis, keepdims=False)
        other = lax.dynamic_index_in_dim(value, 1 - c, axis, keepdims=False)
        got = lax.ppermute(other, "learner", [(0, 1), (1, 0)])
        return (mine.astype(f32) + got.astype(f32)).astype(bf16)

    half = jnp.moveaxis(core_sum(part, 3), 2, 0)
    got = lax.all_to_all(half, "expert", split_axis=0, concat_axis=0, tiled=True)
    total = jnp.sum(got.astype(f32), axis=0)
    hidden = jax.nn.silu(total[:, 0]) * total[:, 1]
    hidden = (hidden * share.reshape(-1)[:, None]).astype(bf16)

    pieces = []
    for turn in range(n_x):
        pairs = []
        for zz in range(n_z):
            for xx in range(n_x):
                for cc in range(n_c):
                    q = zz * n_c + cc
                    owner = (n_dev // n_x) * xx + q // n_x
                    source = (zz * n_x + xx) * n_c + cc
                    target = (owner // n_c * n_x + (q + turn) % n_x) * n_c + owner % n_c
                    pairs.append((source, target))
        pieces.append(lax.ppermute(hidden, ("expert", "replica", "learner"), pairs))
    stack = jnp.stack(pieces)
    order = jnp.mod(x - jnp.arange(n_x), n_x)
    ordered = jnp.take(stack, order, axis=0)
    h = jnp.moveaxis(ordered, 0, 1).reshape(top, n_rows, f_loc)
    wide = jnp.zeros((n_rows, experts, f_loc), bf16)
    for k in range(top):
        wide = wide + jnp.where(picked[k][..., None], h[k][:, None, :], jnp.zeros((), bf16))
    out = jnp.dot(wide.reshape(n_rows, experts * f_loc), w2, preferred_element_type=f32)
    out = out.astype(bf16).reshape(steps, n_z, n_c, rows_dev, cols)
    half = jnp.moveaxis(core_sum(out, 2), 1, 0)
    got = lax.all_to_all(half, "expert", split_axis=0, concat_axis=0, tiled=True)
    return jnp.sum(got.astype(f32), axis=0).astype(bf16)


def body(tokens, gates, expert_ids, gate_up_tiles, gate_up_scales, down_tiles, down_scales):
    steps, rows_dev, width = tokens.shape
    top = expert_ids.shape[2]
    n_z = lax.axis_size("expert")
    n_c = lax.axis_size("learner")
    n_x = lax.axis_size("replica")
    n_dev = n_z * n_c
    z, c, x = lax.axis_index("expert"), lax.axis_index("learner"), lax.axis_index("replica")
    me = z * n_c + c
    experts, d_loc, _, units = gate_up_tiles.shape
    f_loc, cols = down_tiles.shape[1:]
    tile = width // gate_up_scales.shape[1]
    f32, bf16 = jnp.float32, jnp.bfloat16

    def take(scales, axis, first, count):
        index = (first + jnp.arange(count)) // tile
        onehot = (index[:, None] == jnp.arange(scales.shape[axis])[None, :]).astype(f32)
        return jnp.moveaxis(
            jnp.tensordot(scales, onehot, axes=([axis], [1]), precision=lax.Precision.HIGHEST), -1, axis
        )

    s1 = take(take(gate_up_scales, 1, me * d_loc, d_loc), 3, x * units, units)
    w1 = (gate_up_tiles.astype(f32) * s1).astype(bf16)
    s2 = take(down_scales, 1, me * f_loc, f_loc)


    rows = steps * rows_dev
    share = gates / jnp.sum(gates, axis=2, keepdims=True)
    route = jnp.concatenate([expert_ids.astype(f32), share], axis=2).reshape(1, rows, 2 * top)
    sizes = kernel_sizes(n_z, n_c, n_x, top, experts, rows, d_loc, f_loc, units, cols)
    if sizes is None or tile != LANE:
        s2 = take(s2, 2, x * cols, cols)
        w2 = (down_tiles.astype(f32) * s2).astype(bf16)
        route = lax.all_gather(route, ROW_AXES, axis=0, tiled=True)
        return plain(tokens, route, w1, w2, n_x)
    xs = jnp.swapaxes(tokens.reshape(rows, n_dev, d_loc), 0, 1)
    xs = lax.all_to_all(xs, ROW_AXES, split_axis=0, concat_axis=0, tiled=True)
    route = jnp.pad(route[0], ((0, 0), (0, LANE - 2 * top)))
    s2 = lax.dynamic_slice_in_dim(s2, x * (cols // LANE), cols // LANE, 2)
    s2 = jnp.pad(s2, ((0, 0), (0, 0), (0, LANE - cols // LANE)))
    out = fused(sizes, xs, route, s2, jnp.swapaxes(w1, 1, 2), down_tiles)
    return out.reshape(steps, rows_dev, cols)


def solution(mesh):
    placed = (
        P(None, ("group", "expert", "learner"), None),
        P(None, ("group", "expert", "learner"), None),
        P(None, ("group", "expert", "learner"), None),
        P(None, ("expert", "learner"), None, "replica"),
        P(),
        P(None, ("expert", "learner"), "replica"),
        P(),
    )
    return jax.shard_map(
        body,
        mesh=mesh,
        in_specs=placed,
        out_specs=P(None, ("group", "expert", "learner"), "replica"),
        check_vma=False,
    )
```

```python
import functools

import jax
import jax.numpy as jnp
from jax import lax
from jax.experimental import pallas as pl
from jax.experimental.pallas import tpu as pltpu
from jax.sharding import PartitionSpec as P

ROW_AXES = ("expert", "learner")
LANE = 128
OUT_COLS = 512


def shift(index, by, count):
    return lax.rem(index + by, count)


def kernel(sizes, xs, my_route, s2, w1_in, w2_in, out, route, w1, w2, xm, s_send, s_recv, own, z_send, z_recv, z_pass, hid, h_recv,
           wide, q_send, q_recv, q_own, o_send, o_recv, o_pass,
           w1_s, w2_s, r_ss, r_rs, s_ss, s_rs, z_ss, z_rs, z_ps, h_ss, h_fs, h_rs, q_ss, q_rs, o_ss, o_rs, o_ps):
    n_z, n_x, top, experts, rows, d_loc, f_loc, span = sizes
    n_c = 2
    f32, bf16 = jnp.float32, jnp.bfloat16
    z, c, x = lax.axis_index("expert"), lax.axis_index("learner"), lax.axis_index("replica")
    me = z * n_c + c
    chunks = w1.shape[0]
    slots = top * rows
    per_plane = n_z * n_c // n_x
    sibling = {"learner": 1 - c}

    def remote(src, dst, send, recv, device):
        return pltpu.make_async_remote_copy(
            src_ref=src, dst_ref=dst, send_sem=send, recv_sem=recv,
            device_id=device, device_id_type=pl.DeviceIdType.MESH)

    depth = span * LANE

    def w1_copy(n, e, g):
        return pltpu.make_async_copy(
            w1_in.at[e, g, :, pl.ds(pl.multiple_of(n * LANE, LANE), LANE)],
            w1.at[n, pl.ds(e * d_loc, d_loc), pl.ds(g * LANE, LANE)], w1_s.at[n, e, g])

    offset = lax.rem(lax.rem(me, per_plane) * f_loc, LANE)

    def w2_copy(e):
        return pltpu.make_async_copy(
            w2_in.at[e], w2.at[pl.ds(pl.multiple_of(e * depth + offset, 16), f_loc)], w2_s.at[e])

    for n in range(chunks):
        for e in range(experts):
            for g in range(2):
                w1_copy(n, e, g).start()
    for e in range(experts):
        w2_copy(e).start()

    barrier = pltpu.get_barrier_semaphore()
    everyone = n_z * n_c * n_x
    here = (z * n_x + x) * n_c + c
    for turn in range(1, everyone):
        there = shift(here, turn, everyone)
        pl.semaphore_signal(
            barrier, inc=1,
            device_id={"expert": there // (n_x * n_c), "replica": there // n_c % n_x, "learner": there % n_c},
            device_id_type=pl.DeviceIdType.MESH)

    def block_of(half, zz):
        return zz * n_c + (c if half else 1 - c)

    pl.semaphore_wait(barrier, everyone - 1)
    blocks = n_z * n_c

    def route_copy(turn):
        to = shift(me, turn, blocks)
        return remote(my_route, route.at[me], r_ss.at[to], r_rs.at[me],
                      {"expert": to // n_c, "learner": to % n_c})

    def route_arrival(turn):
        source = shift(me, turn, blocks)
        return remote(my_route, route.at[source], r_ss.at[source], r_rs.at[source],
                      {"expert": source // n_c, "learner": source % n_c})

    for turn in range(1, blocks):
        route_copy(turn).start()
    route[me] = my_route[...]
    if depth > f_loc:
        gap = depth - f_loc
        for option in sorted({j * f_loc % LANE for j in range(per_plane)}):
            @pl.when(offset == option)
            def _(option=option):
                for e in range(experts):
                    if option:
                        w2[e * depth:e * depth + option] = jnp.zeros((option, w2.shape[1]), bf16)
                    if gap > option:
                        w2[e * depth + option + f_loc:(e + 1) * depth] = jnp.zeros((gap - option, w2.shape[1]), bf16)
    for turn in range(1, blocks):
        route_arrival(turn).wait_recv()

    for half in range(2):
        for zz in range(n_z):
            p = block_of(half, zz)
            ids = route[p]
            value = xs[p]
            for k in range(top):
                name = jnp.broadcast_to(ids[:, k:k + 1], (rows, d_loc))
                for e in range(experts):
                    xm[half, zz * slots + k * rows:zz * slots + (k + 1) * rows, e * d_loc:(e + 1) * d_loc] = (
                        jnp.where(name == e, value.astype(f32), 0.0).astype(bf16))

    near = z + 1 - 2 * lax.rem(z, 2)
    far_mid = jnp.where(z < 2, 2, 1)
    far_end = jnp.where(z < 2, 3, 0)
    at_end = (z == 0) | (z == n_z - 1)

    def line(send, recv, relay, own, ss, rs, ps):
        def direct(n, block, slot):
            return remote(send.at[n, block], recv.at[n, slot], ss.at[n, block], rs.at[n, slot], {"expert": block})

        def hand(n, block, slot):
            return remote(send.at[n, block], relay.at[n, slot], ss.at[n, block], ps.at[n, slot], {"expert": near})

        def begin(n):
            @pl.when(at_end)
            def _():
                for slot, block in ((1, far_end), (0, far_mid)):
                    send[n, block] = own[n, block].astype(bf16)
                    hand(n, block, slot).start()
            send[n, near] = own[n, near].astype(bf16)
            direct(n, near, 0).start()

        def pass_on(n):
            @pl.when(jnp.logical_not(at_end))
            def _():
                for slot, block in ((1, far_end), (0, far_mid)):
                    hand(n, block, slot).wait_recv()
                    send[n, block] = (own[n, block] + relay[n, slot].astype(f32)).astype(bf16)
                    direct(n, block, 1).start()

        def total(n):
            direct(n, near, 0).wait_recv()
            direct(n, far_mid, 1).wait_recv()
            return own[n, z] + recv[n, 0].astype(f32) + recv[n, 1].astype(f32)

        def close(n):
            for block in (near, far_mid, far_end):
                direct(n, block, 0).wait_send()

        return begin, pass_on, total, close

    def sib_copy(n):
        return remote(s_send.at[n], s_recv.at[n], s_ss.at[n], s_rs.at[n], sibling)

    begin, pass_on, total_of, close = line(z_send, z_recv, z_pass, own, z_ss, z_rs, z_ps)

    def finish(n):
        sib_copy(n).wait_recv()
        own[n] += s_recv[n].astype(f32).reshape(n_z, slots, 2 * LANE)
        begin(n)

    def scale_down(e):
        w2_copy(e).wait()
        band = pl.ds(pl.multiple_of(e * depth + offset, 16), f_loc)
        scales = s2[e]
        for b in range(w2.shape[1] // LANE):
            columns = slice(b * LANE, (b + 1) * LANE)
            w2[band, columns] = (w2[band, columns].astype(f32) * scales[:, b:b + 1]).astype(bf16)

    def step(n, carry):
        for e in range(experts):
            for g in range(2):
                w1_copy(n, e, g).wait()
        s_send[n] = jnp.dot(xm[0], w1[n], preferred_element_type=f32).astype(bf16)
        sib_copy(n).start()
        own[n] = jnp.dot(xm[1], w1[n], preferred_element_type=f32).reshape(n_z, slots, 2 * LANE)

        @pl.when(n > 0)
        def _():
            finish(n - 1)

        @pl.when(n > 1)
        def _():
            pass_on(n - 2)

        @pl.when(n < experts)
        def _():
            scale_down(n)
        return carry

    lax.fori_loop(0, chunks, step, 0)
    finish(chunks - 1)
    for n in range(max(chunks - 2, 0), chunks):
        pass_on(n)

    mine = route[me]

    source_x = me // per_plane

    def h_copy(jj):
        owner = per_plane * x + jj
        first = jj * f_loc // LANE
        return remote(hid.at[pl.ds(first, span)], h_recv.at[me], h_ss.at[jj], h_rs.at[me],
                      {"expert": owner // n_c, "learner": owner % n_c,
                       "replica": jnp.where(c == 0, x, 1 - x)})

    def h_forward(p):
        return remote(h_recv.at[p], h_recv.at[p], h_fs.at[p], h_rs.at[p], {"replica": 1 - x})

    def is_me(jj):
        return (per_plane * x + jj == me) & (c == 0)

    kind = jnp.where(source_x == x, 0, 1)

    def landed(turn):
        return shift(z, turn, n_z) * n_c + kind

    for n in range(chunks):
        total = total_of(n)
        gate, up = total[:, :LANE], total[:, LANE:]
        value = gate / (1.0 + jnp.exp(-gate)) * up
        for k in range(top):
            part = value[k * rows:(k + 1) * rows] * mine[:, top + k:top + k + 1]
            hid[n, k * rows:(k + 1) * rows, :] = part.astype(bf16)
        for jj in range(per_plane):
            first = jj * f_loc // LANE
            if first + span - 1 != n:
                continue
            @pl.when(jnp.logical_not(is_me(jj)))
            def _(jj=jj):
                h_copy(jj).start()

            @pl.when(is_me(jj))
            def _(first=first):
                h_recv[me] = hid[first:first + span]

    for turn in range(n_z):
        p = landed(turn)

        @pl.when(jnp.logical_not((p == me) & (kind == 0)))
        def _(p=p):
            h_forward(p).wait_recv()

        h_forward(p).start()
    for turn in range(n_z):
        h_forward(shift(z, turn, n_z) * n_c + 1 - kind).wait_recv()

    for half in range(2):
        for zz in range(n_z):
            p = block_of(half, zz)
            ids = route[p]
            for e in range(experts):
                for s in range(span):
                    value = jnp.zeros((rows, LANE), f32)
                    for k in range(top):
                        name = jnp.broadcast_to(ids[:, k:k + 1], (rows, LANE))
                        value = value + jnp.where(name == e, h_recv[p, s, k * rows:(k + 1) * rows, :].astype(f32), 0.0)
                    wide[half, zz * rows:(zz + 1) * rows, e * depth + s * LANE:e * depth + (s + 1) * LANE] = value.astype(bf16)

    def q_copy(n):
        return remote(q_send.at[n], q_recv.at[n], q_ss.at[n], q_rs.at[n], sibling)

    begin_out, pass_out, total_out, close_out = line(o_send, o_recv, o_pass, q_own, o_ss, o_rs, o_ps)

    def finish_out(n):
        q_copy(n).wait_recv()
        q_own[n] += q_recv[n].astype(f32).reshape(n_z, rows, OUT_COLS)
        begin_out(n)

    out_chunks = w2.shape[1] // OUT_COLS
    for e in range(chunks, experts):
        scale_down(e)

    def step_out(n, carry):
        columns = pl.ds(pl.multiple_of(n * OUT_COLS, OUT_COLS), OUT_COLS)
        q_send[n] = jnp.dot(wide[0], w2[:, columns], preferred_element_type=f32).astype(bf16)
        q_copy(n).start()
        q_own[n] = jnp.dot(wide[1], w2[:, columns], preferred_element_type=f32).reshape(n_z, rows, OUT_COLS)

        @pl.when(n > 0)
        def _():
            finish_out(n - 1)

        @pl.when(n > 1)
        def _():
            pass_out(n - 2)
        return carry

    lax.fori_loop(0, out_chunks, step_out, 0)
    finish_out(out_chunks - 1)
    for n in range(max(out_chunks - 2, 0), out_chunks):
        pass_out(n)

    for n in range(out_chunks):
        out[:, n * OUT_COLS:(n + 1) * OUT_COLS] = total_out(n).astype(bf16)

    for turn in range(1, blocks):
        route_copy(turn).wait_send()
    for n in range(chunks):
        sib_copy(n).wait_send()
        close(n)
    for jj in range(per_plane):
        @pl.when(jnp.logical_not(is_me(jj)))
        def _(jj=jj):
            h_copy(jj).wait_send()

    for turn in range(n_z):
        h_forward(landed(turn)).wait_send()
    for n in range(out_chunks):
        q_copy(n).wait_send()
        close_out(n)


def fused(sizes, xs, route, s2, w1, w2):
    n_z, n_x, top, experts, rows, d_loc, f_loc, span = sizes
    n_dev = 2 * n_z
    chunks, cols = w1.shape[3] // LANE, w2.shape[2]
    slots = top * rows
    out_chunks = cols // OUT_COLS
    bf16, f32 = jnp.bfloat16, jnp.float32
    vmem, dma = pltpu.VMEM, pltpu.SemaphoreType.DMA
    per_plane = n_dev // n_x
    return pl.pallas_call(
        functools.partial(kernel, sizes),
        out_shape=jax.ShapeDtypeStruct((rows, cols), bf16),
        in_specs=[pl.BlockSpec(memory_space=pltpu.VMEM)] * 3 + [pl.BlockSpec(memory_space=pl.ANY)] * 2,
        out_specs=pl.BlockSpec(memory_space=pltpu.VMEM),
        scratch_shapes=[
            vmem((n_dev, rows, LANE), f32),
            vmem((chunks, experts * d_loc, 2 * LANE), bf16),
            vmem((experts * span * LANE, cols), bf16),
            vmem((2, n_z * slots, experts * d_loc), bf16),
            vmem((chunks, n_z * slots, 2 * LANE), bf16),
            vmem((chunks, n_z * slots, 2 * LANE), bf16),
            vmem((chunks, n_z, slots, 2 * LANE), f32),
            vmem((chunks, n_z, slots, 2 * LANE), bf16),
            vmem((chunks, 2, slots, 2 * LANE), bf16),
            vmem((chunks, 2, slots, 2 * LANE), bf16),
            vmem((chunks, slots, LANE), bf16),
            vmem((n_dev, span, slots, LANE), bf16),
            vmem((2, n_z * rows, experts * span * LANE), bf16),
            vmem((out_chunks, n_z * rows, OUT_COLS), bf16),
            vmem((out_chunks, n_z * rows, OUT_COLS), bf16),
            vmem((out_chunks, n_z, rows, OUT_COLS), f32),
            vmem((out_chunks, n_z, rows, OUT_COLS), bf16),
            vmem((out_chunks, 2, rows, OUT_COLS), bf16),
            vmem((out_chunks, 2, rows, OUT_COLS), bf16),
            dma((chunks, experts, 2)), dma((experts,)),
            dma((n_dev,)), dma((n_dev,)),
            dma((chunks,)), dma((chunks,)),
            dma((chunks, n_z)), dma((chunks, 2)), dma((chunks, 2)),
            dma((per_plane,)), dma((n_dev,)), dma((n_dev,)),
            dma((out_chunks,)), dma((out_chunks,)),
            dma((out_chunks, n_z)), dma((out_chunks, 2)), dma((out_chunks, 2)),
        ],
        compiler_params=pltpu.CompilerParams(
            collective_id=0, has_side_effects=True, vmem_limit_bytes=58 * 1024 * 1024),
    )(xs, route, s2, w1, w2)


def kernel_sizes(n_z, n_c, n_x, top, experts, rows, d_loc, f_loc, units, cols):
    if n_x != 2 or n_z != 4 or n_c != 2 or units % LANE or cols % OUT_COLS or rows % 16 or (n_z * n_c) % n_x:
        return None
    spans = [-(-((j + 1) * f_loc) // LANE) - j * f_loc // LANE for j in range(n_z * n_c // n_x)]
    span = max(spans)
    chunks = units // LANE
    if any(j * f_loc // LANE + span > chunks for j in range(len(spans))):
        return None
    if 2 * n_z * top * rows * experts * d_loc * 2 > 8 * 1024 * 1024:
        return None
    return n_z, n_x, top, experts, rows, d_loc, f_loc, span


def plain(tokens, route, w1, w2, n_x):
    f32, bf16 = jnp.float32, jnp.bfloat16
    n_z, n_c = lax.axis_size("expert"), lax.axis_size("learner")
    c, x = lax.axis_index("learner"), lax.axis_index("replica")
    n_dev = n_z * n_c
    steps, rows_dev, _ = tokens.shape
    experts, d_loc, _, units = w1.shape
    f_loc, cols = w2.shape[1:]
    top = route.shape[2] // 2
    piece = units // n_dev
    n_rows = steps * rows_dev * n_dev
    xs = lax.all_to_all(tokens, ROW_AXES, split_axis=2, concat_axis=1, tiled=True).reshape(n_rows, d_loc)
    route = route.reshape(n_dev, steps, rows_dev, 2 * top).swapaxes(0, 1).reshape(n_rows, 2 * top)
    ids = route[:, :top].T.astype(jnp.int32)
    share = route[:, top:].T
    w1 = w1.reshape(experts * d_loc, 2 * units)
    w2 = w2.reshape(experts * f_loc, cols)
    names = jnp.arange(experts, dtype=jnp.int32)
    picked = ids[:, :, None] == names
    masked = jnp.where(picked[..., None], xs[None, :, None, :], jnp.zeros((), bf16))
    part = jnp.dot(masked.reshape(top * n_rows, experts * d_loc), w1, preferred_element_type=f32)
    part = part.astype(bf16).reshape(top * n_rows, 2, n_z, n_c, piece)

    def core_sum(value, axis):
        mine = lax.dynamic_index_in_dim(value, c, axis, keepdims=False)
        other = lax.dynamic_index_in_dim(value, 1 - c, axis, keepdims=False)
        got = lax.ppermute(other, "learner", [(0, 1), (1, 0)])
        return (mine.astype(f32) + got.astype(f32)).astype(bf16)

    half = jnp.moveaxis(core_sum(part, 3), 2, 0)
    got = lax.all_to_all(half, "expert", split_axis=0, concat_axis=0, tiled=True)
    total = jnp.sum(got.astype(f32), axis=0)
    hidden = jax.nn.silu(total[:, 0]) * total[:, 1]
    hidden = (hidden * share.reshape(-1)[:, None]).astype(bf16)

    pieces = []
    for turn in range(n_x):
        pairs = []
        for zz in range(n_z):
            for xx in range(n_x):
                for cc in range(n_c):
                    q = zz * n_c + cc
                    owner = (n_dev // n_x) * xx + q // n_x
                    source = (zz * n_x + xx) * n_c + cc
                    target = (owner // n_c * n_x + (q + turn) % n_x) * n_c + owner % n_c
                    pairs.append((source, target))
        pieces.append(lax.ppermute(hidden, ("expert", "replica", "learner"), pairs))
    stack = jnp.stack(pieces)
    order = jnp.mod(x - jnp.arange(n_x), n_x)
    ordered = jnp.take(stack, order, axis=0)
    h = jnp.moveaxis(ordered, 0, 1).reshape(top, n_rows, f_loc)
    wide = jnp.zeros((n_rows, experts, f_loc), bf16)
    for k in range(top):
        wide = wide + jnp.where(picked[k][..., None], h[k][:, None, :], jnp.zeros((), bf16))
    out = jnp.dot(wide.reshape(n_rows, experts * f_loc), w2, preferred_element_type=f32)
    out = out.astype(bf16).reshape(steps, n_z, n_c, rows_dev, cols)
    half = jnp.moveaxis(core_sum(out, 2), 1, 0)
    got = lax.all_to_all(half, "expert", split_axis=0, concat_axis=0, tiled=True)
    return jnp.sum(got.astype(f32), axis=0).astype(bf16)


def body(tokens, gates, expert_ids, gate_up_tiles, gate_up_scales, down_tiles, down_scales):
    steps, rows_dev, width = tokens.shape
    top = expert_ids.shape[2]
    n_z = lax.axis_size("expert")
    n_c = lax.axis_size("learner")
    n_x = lax.axis_size("replica")
    n_dev = n_z * n_c
    z, c, x = lax.axis_index("expert"), lax.axis_index("learner"), lax.axis_index("replica")
    me = z * n_c + c
    experts, d_loc, _, units = gate_up_tiles.shape
    f_loc, cols = down_tiles.shape[1:]
    tile = width // gate_up_scales.shape[1]
    f32, bf16 = jnp.float32, jnp.bfloat16

    def take(scales, axis, first, count):
        index = (first + jnp.arange(count)) // tile
        onehot = (index[:, None] == jnp.arange(scales.shape[axis])[None, :]).astype(f32)
        return jnp.moveaxis(
            jnp.tensordot(scales, onehot, axes=([axis], [1]), precision=lax.Precision.HIGHEST), -1, axis
        )

    s1 = take(take(gate_up_scales, 1, me * d_loc, d_loc), 3, x * units, units)
    w1 = (gate_up_tiles.astype(f32) * s1).astype(bf16)
    s2 = take(down_scales, 1, me * f_loc, f_loc)


    rows = steps * rows_dev
    share = gates / jnp.sum(gates, axis=2, keepdims=True)
    route = jnp.concatenate([expert_ids.astype(f32), share], axis=2).reshape(1, rows, 2 * top)
    sizes = kernel_sizes(n_z, n_c, n_x, top, experts, rows, d_loc, f_loc, units, cols)
    if sizes is None or tile != LANE:
        s2 = take(s2, 2, x * cols, cols)
        w2 = (down_tiles.astype(f32) * s2).astype(bf16)
        route = lax.all_gather(route, ROW_AXES, axis=0, tiled=True)
        return plain(tokens, route, w1, w2, n_x)
    xs = jnp.swapaxes(tokens.reshape(rows, n_dev, d_loc), 0, 1)
    xs = lax.all_to_all(xs, ROW_AXES, split_axis=0, concat_axis=0, tiled=True)
    route = jnp.pad(route[0], ((0, 0), (0, LANE - 2 * top)))
    s2 = lax.dynamic_slice_in_dim(s2, x * (cols // LANE), cols // LANE, 2)
    s2 = jnp.pad(s2, ((0, 0), (0, 0), (0, LANE - cols // LANE)))
    out = fused(sizes, xs, route, s2, jnp.swapaxes(w1, 1, 2), down_tiles)
    return out.reshape(steps, rows_dev, cols)


def solution(mesh):
    placed = (
        P(None, ("group", "expert", "learner"), None),
        P(None, ("group", "expert", "learner"), None),
        P(None, ("group", "expert", "learner"), None),
        P(None, ("expert", "learner"), None, "replica"),
        P(),
        P(None, ("expert", "learner"), "replica"),
        P(),
    )
    return jax.shard_map(
        body,
        mesh=mesh,
        in_specs=placed,
        out_specs=P(None, ("group", "expert", "learner"), "replica"),
        check_vma=False,
    )
```

```python
import functools

import jax
import jax.numpy as jnp
from jax import lax
from jax.experimental import pallas as pl
from jax.experimental.pallas import tpu as pltpu
from jax.sharding import PartitionSpec as P

ROW_AXES = ("expert", "learner")
LANE = 128
OUT_COLS = 256


def shift(index, by, count):
    return lax.rem(index + by, count)


def kernel(sizes, xs, my_route, s2, w1_in, w2_in, out, route, w1, w2, xm, s_send, s_recv, own, z_send, z_recv, z_pass, hid, h_recv,
           wide, q_send, q_recv, q_own, o_send, o_recv, o_pass,
           w1_s, w2_s, r_ss, r_rs, s_ss, s_rs, z_ss, z_rs, z_ps, h_ss, h_fs, h_rs, q_ss, q_rs, o_ss, o_rs, o_ps):
    n_z, n_x, top, experts, rows, d_loc, f_loc, span = sizes
    n_c = 2
    f32, bf16 = jnp.float32, jnp.bfloat16
    z, c, x = lax.axis_index("expert"), lax.axis_index("learner"), lax.axis_index("replica")
    me = z * n_c + c
    chunks = w1.shape[0]
    slots = top * rows
    per_plane = n_z * n_c // n_x
    sibling = {"learner": 1 - c}

    def remote(src, dst, send, recv, device):
        return pltpu.make_async_remote_copy(
            src_ref=src, dst_ref=dst, send_sem=send, recv_sem=recv,
            device_id=device, device_id_type=pl.DeviceIdType.MESH)

    depth = span * LANE

    def w1_copy(n, e, g):
        return pltpu.make_async_copy(
            w1_in.at[e, g, :, pl.ds(pl.multiple_of(n * LANE, LANE), LANE)],
            w1.at[n, pl.ds(e * d_loc, d_loc), pl.ds(g * LANE, LANE)], w1_s.at[n, e, g])

    offset = lax.rem(lax.rem(me, per_plane) * f_loc, LANE)

    def w2_copy(e):
        return pltpu.make_async_copy(
            w2_in.at[e], w2.at[pl.ds(pl.multiple_of(e * depth + offset, 16), f_loc)], w2_s.at[e])

    for n in range(chunks):
        for e in range(experts):
            for g in range(2):
                w1_copy(n, e, g).start()
    for e in range(experts):
        w2_copy(e).start()

    barrier = pltpu.get_barrier_semaphore()
    everyone = n_z * n_c * n_x
    here = (z * n_x + x) * n_c + c
    for turn in range(1, everyone):
        there = shift(here, turn, everyone)
        pl.semaphore_signal(
            barrier, inc=1,
            device_id={"expert": there // (n_x * n_c), "replica": there // n_c % n_x, "learner": there % n_c},
            device_id_type=pl.DeviceIdType.MESH)

    def block_of(half, zz):
        return zz * n_c + (c if half else 1 - c)

    pl.semaphore_wait(barrier, everyone - 1)
    blocks = n_z * n_c

    def route_copy(turn):
        to = shift(me, turn, blocks)
        return remote(my_route, route.at[me], r_ss.at[to], r_rs.at[me],
                      {"expert": to // n_c, "learner": to % n_c})

    def route_arrival(turn):
        source = shift(me, turn, blocks)
        return remote(my_route, route.at[source], r_ss.at[source], r_rs.at[source],
                      {"expert": source // n_c, "learner": source % n_c})

    for turn in range(1, blocks):
        route_copy(turn).start()
    route[me] = my_route[...]
    if depth > f_loc:
        gap = depth - f_loc
        for option in sorted({j * f_loc % LANE for j in range(per_plane)}):
            @pl.when(offset == option)
            def _(option=option):
                for e in range(experts):
                    if option:
                        w2[e * depth:e * depth + option] = jnp.zeros((option, w2.shape[1]), bf16)
                    if gap > option:
                        w2[e * depth + option + f_loc:(e + 1) * depth] = jnp.zeros((gap - option, w2.shape[1]), bf16)
    for turn in range(1, blocks):
        route_arrival(turn).wait_recv()

    for half in range(2):
        for zz in range(n_z):
            p = block_of(half, zz)
            ids = route[p]
            value = xs[p]
            for k in range(top):
                name = jnp.broadcast_to(ids[:, k:k + 1], (rows, d_loc))
                for e in range(experts):
                    xm[half, zz * slots + k * rows:zz * slots + (k + 1) * rows, e * d_loc:(e + 1) * d_loc] = (
                        jnp.where(name == e, value.astype(f32), 0.0).astype(bf16))

    near = z + 1 - 2 * lax.rem(z, 2)
    far_mid = jnp.where(z < 2, 2, 1)
    far_end = jnp.where(z < 2, 3, 0)
    at_end = (z == 0) | (z == n_z - 1)

    def line(send, recv, relay, own, ss, rs, ps):
        def direct(n, block, slot):
            return remote(send.at[n, block], recv.at[n, slot], ss.at[n, block], rs.at[n, slot], {"expert": block})

        def hand(n, block, slot):
            return remote(send.at[n, block], relay.at[n, slot], ss.at[n, block], ps.at[n, slot], {"expert": near})

        def begin(n):
            @pl.when(at_end)
            def _():
                for slot, block in ((1, far_end), (0, far_mid)):
                    send[n, block] = own[n, block].astype(bf16)
                    hand(n, block, slot).start()
            send[n, near] = own[n, near].astype(bf16)
            direct(n, near, 0).start()

        def pass_on(n):
            @pl.when(jnp.logical_not(at_end))
            def _():
                for slot, block in ((1, far_end), (0, far_mid)):
                    hand(n, block, slot).wait_recv()
                    send[n, block] = (own[n, block] + relay[n, slot].astype(f32)).astype(bf16)
                    direct(n, block, 1).start()

        def total(n):
            direct(n, near, 0).wait_recv()
            direct(n, far_mid, 1).wait_recv()
            return own[n, z] + recv[n, 0].astype(f32) + recv[n, 1].astype(f32)

        def close(n):
            for block in (near, far_mid, far_end):
                direct(n, block, 0).wait_send()

        return begin, pass_on, total, close

    def sib_copy(n):
        return remote(s_send.at[n], s_recv.at[n], s_ss.at[n], s_rs.at[n], sibling)

    begin, pass_on, total_of, close = line(z_send, z_recv, z_pass, own, z_ss, z_rs, z_ps)

    def finish(n):
        sib_copy(n).wait_recv()
        own[n] += s_recv[n].astype(f32).reshape(n_z, slots, 2 * LANE)
        begin(n)

    def scale_down(e):
        w2_copy(e).wait()
        band = pl.ds(pl.multiple_of(e * depth + offset, 16), f_loc)
        scales = s2[e]
        for b in range(w2.shape[1] // LANE):
            columns = slice(b * LANE, (b + 1) * LANE)
            w2[band, columns] = (w2[band, columns].astype(f32) * scales[:, b:b + 1]).astype(bf16)

    def step(n, carry):
        for e in range(experts):
            for g in range(2):
                w1_copy(n, e, g).wait()
        s_send[n] = jnp.dot(xm[0], w1[n], preferred_element_type=f32).astype(bf16)
        sib_copy(n).start()
        own[n] = jnp.dot(xm[1], w1[n], preferred_element_type=f32).reshape(n_z, slots, 2 * LANE)

        @pl.when(n > 0)
        def _():
            finish(n - 1)

        @pl.when(n > 1)
        def _():
            pass_on(n - 2)

        @pl.when(n < experts)
        def _():
            scale_down(n)
        return carry

    lax.fori_loop(0, chunks, step, 0)
    finish(chunks - 1)
    for n in range(max(chunks - 2, 0), chunks):
        pass_on(n)

    mine = route[me]

    source_x = me // per_plane

    def h_copy(jj):
        owner = per_plane * x + jj
        first = jj * f_loc // LANE
        return remote(hid.at[pl.ds(first, span)], h_recv.at[me], h_ss.at[jj], h_rs.at[me],
                      {"expert": owner // n_c, "learner": owner % n_c,
                       "replica": jnp.where(c == 0, x, 1 - x)})

    def h_forward(p):
        return remote(h_recv.at[p], h_recv.at[p], h_fs.at[p], h_rs.at[p], {"replica": 1 - x})

    def is_me(jj):
        return (per_plane * x + jj == me) & (c == 0)

    kind = jnp.where(source_x == x, 0, 1)

    def landed(turn):
        return shift(z, turn, n_z) * n_c + kind

    for n in range(chunks):
        total = total_of(n)
        gate, up = total[:, :LANE], total[:, LANE:]
        value = gate / (1.0 + jnp.exp(-gate)) * up
        for k in range(top):
            part = value[k * rows:(k + 1) * rows] * mine[:, top + k:top + k + 1]
            hid[n, k * rows:(k + 1) * rows, :] = part.astype(bf16)
        for jj in range(per_plane):
            first = jj * f_loc // LANE
            if first + span - 1 != n:
                continue
            @pl.when(jnp.logical_not(is_me(jj)))
            def _(jj=jj):
                h_copy(jj).start()

            @pl.when(is_me(jj))
            def _(first=first):
                h_recv[me] = hid[first:first + span]

    for turn in range(n_z):
        p = landed(turn)

        @pl.when(jnp.logical_not((p == me) & (kind == 0)))
        def _(p=p):
            h_forward(p).wait_recv()

        h_forward(p).start()
    for turn in range(n_z):
        h_forward(shift(z, turn, n_z) * n_c + 1 - kind).wait_recv()

    for half in range(2):
        for zz in range(n_z):
            p = block_of(half, zz)
            ids = route[p]
            for e in range(experts):
                for s in range(span):
                    value = jnp.zeros((rows, LANE), f32)
                    for k in range(top):
                        name = jnp.broadcast_to(ids[:, k:k + 1], (rows, LANE))
                        value = value + jnp.where(name == e, h_recv[p, s, k * rows:(k + 1) * rows, :].astype(f32), 0.0)
                    wide[half, zz * rows:(zz + 1) * rows, e * depth + s * LANE:e * depth + (s + 1) * LANE] = value.astype(bf16)

    def q_copy(n):
        return remote(q_send.at[n], q_recv.at[n], q_ss.at[n], q_rs.at[n], sibling)

    begin_out, pass_out, total_out, close_out = line(o_send, o_recv, o_pass, q_own, o_ss, o_rs, o_ps)

    def finish_out(n):
        q_copy(n).wait_recv()
        q_own[n] += q_recv[n].astype(f32).reshape(n_z, rows, OUT_COLS)
        begin_out(n)

    out_chunks = w2.shape[1] // OUT_COLS
    for e in range(chunks, experts):
        scale_down(e)

    def step_out(n, carry):
        columns = pl.ds(pl.multiple_of(n * OUT_COLS, OUT_COLS), OUT_COLS)
        q_send[n] = jnp.dot(wide[0], w2[:, columns], preferred_element_type=f32).astype(bf16)
        q_copy(n).start()
        q_own[n] = jnp.dot(wide[1], w2[:, columns], preferred_element_type=f32).reshape(n_z, rows, OUT_COLS)

        @pl.when(n > 0)
        def _():
            finish_out(n - 1)

        @pl.when(n > 1)
        def _():
            pass_out(n - 2)
        return carry

    lax.fori_loop(0, out_chunks, step_out, 0)
    finish_out(out_chunks - 1)
    for n in range(max(out_chunks - 2, 0), out_chunks):
        pass_out(n)

    for n in range(out_chunks):
        out[:, n * OUT_COLS:(n + 1) * OUT_COLS] = total_out(n).astype(bf16)

    for turn in range(1, blocks):
        route_copy(turn).wait_send()
    for n in range(chunks):
        sib_copy(n).wait_send()
        close(n)
    for jj in range(per_plane):
        @pl.when(jnp.logical_not(is_me(jj)))
        def _(jj=jj):
            h_copy(jj).wait_send()

    for turn in range(n_z):
        h_forward(landed(turn)).wait_send()
    for n in range(out_chunks):
        q_copy(n).wait_send()
        close_out(n)


def fused(sizes, xs, route, s2, w1, w2):
    n_z, n_x, top, experts, rows, d_loc, f_loc, span = sizes
    n_dev = 2 * n_z
    chunks, cols = w1.shape[3] // LANE, w2.shape[2]
    slots = top * rows
    out_chunks = cols // OUT_COLS
    bf16, f32 = jnp.bfloat16, jnp.float32
    vmem, dma = pltpu.VMEM, pltpu.SemaphoreType.DMA
    per_plane = n_dev // n_x
    return pl.pallas_call(
        functools.partial(kernel, sizes),
        out_shape=jax.ShapeDtypeStruct((rows, cols), bf16),
        in_specs=[pl.BlockSpec(memory_space=pltpu.VMEM)] * 3 + [pl.BlockSpec(memory_space=pl.ANY)] * 2,
        out_specs=pl.BlockSpec(memory_space=pltpu.VMEM),
        scratch_shapes=[
            vmem((n_dev, rows, LANE), f32),
            vmem((chunks, experts * d_loc, 2 * LANE), bf16),
            vmem((experts * span * LANE, cols), bf16),
            vmem((2, n_z * slots, experts * d_loc), bf16),
            vmem((chunks, n_z * slots, 2 * LANE), bf16),
            vmem((chunks, n_z * slots, 2 * LANE), bf16),
            vmem((chunks, n_z, slots, 2 * LANE), f32),
            vmem((chunks, n_z, slots, 2 * LANE), bf16),
            vmem((chunks, 2, slots, 2 * LANE), bf16),
            vmem((chunks, 2, slots, 2 * LANE), bf16),
            vmem((chunks, slots, LANE), bf16),
            vmem((n_dev, span, slots, LANE), bf16),
            vmem((2, n_z * rows, experts * span * LANE), bf16),
            vmem((out_chunks, n_z * rows, OUT_COLS), bf16),
            vmem((out_chunks, n_z * rows, OUT_COLS), bf16),
            vmem((out_chunks, n_z, rows, OUT_COLS), f32),
            vmem((out_chunks, n_z, rows, OUT_COLS), bf16),
            vmem((out_chunks, 2, rows, OUT_COLS), bf16),
            vmem((out_chunks, 2, rows, OUT_COLS), bf16),
            dma((chunks, experts, 2)), dma((experts,)),
            dma((n_dev,)), dma((n_dev,)),
            dma((chunks,)), dma((chunks,)),
            dma((chunks, n_z)), dma((chunks, 2)), dma((chunks, 2)),
            dma((per_plane,)), dma((n_dev,)), dma((n_dev,)),
            dma((out_chunks,)), dma((out_chunks,)),
            dma((out_chunks, n_z)), dma((out_chunks, 2)), dma((out_chunks, 2)),
        ],
        compiler_params=pltpu.CompilerParams(
            collective_id=0, has_side_effects=True, vmem_limit_bytes=58 * 1024 * 1024),
    )(xs, route, s2, w1, w2)


def kernel_sizes(n_z, n_c, n_x, top, experts, rows, d_loc, f_loc, units, cols):
    if n_x != 2 or n_z != 4 or n_c != 2 or units % LANE or cols % OUT_COLS or rows % 16 or (n_z * n_c) % n_x:
        return None
    spans = [-(-((j + 1) * f_loc) // LANE) - j * f_loc // LANE for j in range(n_z * n_c // n_x)]
    span = max(spans)
    chunks = units // LANE
    if any(j * f_loc // LANE + span > chunks for j in range(len(spans))):
        return None
    if 2 * n_z * top * rows * experts * d_loc * 2 > 8 * 1024 * 1024:
        return None
    return n_z, n_x, top, experts, rows, d_loc, f_loc, span


def plain(tokens, route, w1, w2, n_x):
    f32, bf16 = jnp.float32, jnp.bfloat16
    n_z, n_c = lax.axis_size("expert"), lax.axis_size("learner")
    c, x = lax.axis_index("learner"), lax.axis_index("replica")
    n_dev = n_z * n_c
    steps, rows_dev, _ = tokens.shape
    experts, d_loc, _, units = w1.shape
    f_loc, cols = w2.shape[1:]
    top = route.shape[2] // 2
    piece = units // n_dev
    n_rows = steps * rows_dev * n_dev
    xs = lax.all_to_all(tokens, ROW_AXES, split_axis=2, concat_axis=1, tiled=True).reshape(n_rows, d_loc)
    route = route.reshape(n_dev, steps, rows_dev, 2 * top).swapaxes(0, 1).reshape(n_rows, 2 * top)
    ids = route[:, :top].T.astype(jnp.int32)
    share = route[:, top:].T
    w1 = w1.reshape(experts * d_loc, 2 * units)
    w2 = w2.reshape(experts * f_loc, cols)
    names = jnp.arange(experts, dtype=jnp.int32)
    picked = ids[:, :, None] == names
    masked = jnp.where(picked[..., None], xs[None, :, None, :], jnp.zeros((), bf16))
    part = jnp.dot(masked.reshape(top * n_rows, experts * d_loc), w1, preferred_element_type=f32)
    part = part.astype(bf16).reshape(top * n_rows, 2, n_z, n_c, piece)

    def core_sum(value, axis):
        mine = lax.dynamic_index_in_dim(value, c, axis, keepdims=False)
        other = lax.dynamic_index_in_dim(value, 1 - c, axis, keepdims=False)
        got = lax.ppermute(other, "learner", [(0, 1), (1, 0)])
        return (mine.astype(f32) + got.astype(f32)).astype(bf16)

    half = jnp.moveaxis(core_sum(part, 3), 2, 0)
    got = lax.all_to_all(half, "expert", split_axis=0, concat_axis=0, tiled=True)
    total = jnp.sum(got.astype(f32), axis=0)
    hidden = jax.nn.silu(total[:, 0]) * total[:, 1]
    hidden = (hidden * share.reshape(-1)[:, None]).astype(bf16)

    pieces = []
    for turn in range(n_x):
        pairs = []
        for zz in range(n_z):
            for xx in range(n_x):
                for cc in range(n_c):
                    q = zz * n_c + cc
                    owner = (n_dev // n_x) * xx + q // n_x
                    source = (zz * n_x + xx) * n_c + cc
                    target = (owner // n_c * n_x + (q + turn) % n_x) * n_c + owner % n_c
                    pairs.append((source, target))
        pieces.append(lax.ppermute(hidden, ("expert", "replica", "learner"), pairs))
    stack = jnp.stack(pieces)
    order = jnp.mod(x - jnp.arange(n_x), n_x)
    ordered = jnp.take(stack, order, axis=0)
    h = jnp.moveaxis(ordered, 0, 1).reshape(top, n_rows, f_loc)
    wide = jnp.zeros((n_rows, experts, f_loc), bf16)
    for k in range(top):
        wide = wide + jnp.where(picked[k][..., None], h[k][:, None, :], jnp.zeros((), bf16))
    out = jnp.dot(wide.reshape(n_rows, experts * f_loc), w2, preferred_element_type=f32)
    out = out.astype(bf16).reshape(steps, n_z, n_c, rows_dev, cols)
    half = jnp.moveaxis(core_sum(out, 2), 1, 0)
    got = lax.all_to_all(half, "expert", split_axis=0, concat_axis=0, tiled=True)
    return jnp.sum(got.astype(f32), axis=0).astype(bf16)


def body(tokens, gates, expert_ids, gate_up_tiles, gate_up_scales, down_tiles, down_scales):
    steps, rows_dev, width = tokens.shape
    top = expert_ids.shape[2]
    n_z = lax.axis_size("expert")
    n_c = lax.axis_size("learner")
    n_x = lax.axis_size("replica")
    n_dev = n_z * n_c
    z, c, x = lax.axis_index("expert"), lax.axis_index("learner"), lax.axis_index("replica")
    me = z * n_c + c
    experts, d_loc, _, units = gate_up_tiles.shape
    f_loc, cols = down_tiles.shape[1:]
    tile = width // gate_up_scales.shape[1]
    f32, bf16 = jnp.float32, jnp.bfloat16

    def take(scales, axis, first, count):
        index = (first + jnp.arange(count)) // tile
        onehot = (index[:, None] == jnp.arange(scales.shape[axis])[None, :]).astype(f32)
        return jnp.moveaxis(
            jnp.tensordot(scales, onehot, axes=([axis], [1]), precision=lax.Precision.HIGHEST), -1, axis
        )

    s1 = take(take(gate_up_scales, 1, me * d_loc, d_loc), 3, x * units, units)
    w1 = (gate_up_tiles.astype(f32) * s1).astype(bf16)
    s2 = take(down_scales, 1, me * f_loc, f_loc)


    rows = steps * rows_dev
    share = gates / jnp.sum(gates, axis=2, keepdims=True)
    route = jnp.concatenate([expert_ids.astype(f32), share], axis=2).reshape(1, rows, 2 * top)
    sizes = kernel_sizes(n_z, n_c, n_x, top, experts, rows, d_loc, f_loc, units, cols)
    if sizes is None or tile != LANE:
        s2 = take(s2, 2, x * cols, cols)
        w2 = (down_tiles.astype(f32) * s2).astype(bf16)
        route = lax.all_gather(route, ROW_AXES, axis=0, tiled=True)
        return plain(tokens, route, w1, w2, n_x)
    xs = jnp.swapaxes(tokens.reshape(rows, n_dev, d_loc), 0, 1)
    xs = lax.all_to_all(xs, ROW_AXES, split_axis=0, concat_axis=0, tiled=True)
    route = jnp.pad(route[0], ((0, 0), (0, LANE - 2 * top)))
    s2 = lax.dynamic_slice_in_dim(s2, x * (cols // LANE), cols // LANE, 2)
    s2 = jnp.pad(s2, ((0, 0), (0, 0), (0, LANE - cols // LANE)))
    out = fused(sizes, xs, route, s2, jnp.swapaxes(w1, 1, 2), down_tiles)
    return out.reshape(steps, rows_dev, cols)


def solution(mesh):
    placed = (
        P(None, ("group", "expert", "learner"), None),
        P(None, ("group", "expert", "learner"), None),
        P(None, ("group", "expert", "learner"), None),
        P(None, ("expert", "learner"), None, "replica"),
        P(),
        P(None, ("expert", "learner"), "replica"),
        P(),
    )
    return jax.shard_map(
        body,
        mesh=mesh,
        in_specs=placed,
        out_specs=P(None, ("group", "expert", "learner"), "replica"),
        check_vma=False,
    )
```
